128 devices in a mesh: dp: 4 (over y), ctx: 8 (over z, core), head: 4 (over x).
Axes of the slice: x: 4, y: 4, z: 4, core: 2. Of those that a mesh axis runs over, the one named last changes fastest.
Arguments:
- queries: bfloat16 [12288, 12288], P(('dp', 'ctx'), 'head'), parts along dimension 0, may hold values from -12 to 12
- latent: bfloat16 [12288, 576], P(('dp', 'ctx', 'head')), parts along dimension 0, may hold values from -6 to 6
- segments: int32 [12288], P('dp'), parts along dimension 0, may hold values from 0 to 11, never falling along the last dimension, each value on 1 to 1536 neighbouring positions
- w_uk: bfloat16 [64, 128, 512], P('head'), may hold values from -0.5 to 0.5
- w_uv: bfloat16 [64, 512, 128], P('head'), may hold values from -0.25 to 0.25
Outputs:
- attended: bfloat16 [12288, 8192], P(('dp', 'ctx'), 'head'), parts along dimension 0
The draws below stay inside these ranges and needn't reach their ends.
There are 4 independent parts, one for each index of `dp`. The reference program is written for one: setup_inputs(seed, part) draws one part's arguments, and reference() takes and returns one part's arrays. A program takes and returns all parts, laid end to end along the dimension named above; an argument that names none is the same for every part. Nothing has to cross between parts.
Inputs may be any that keep to these rules, and one draw needn't show every extreme that they name: `segments`: document numbers never fall along the sequence; each document has 1 to 1536 positions and one has exactly 1536.
All inputs are finite; a program needn't handle non-finite values.
Results may differ from the reference program's by a relative error of at most 0.0065.
Values may be sent and summed in bfloat16 or wider, within the bound.
No kernel may reach another device: no remote copies, remote signals or barrier semaphores. Data moves between devices by JAX's collectives and lax.ppermute only.
A program may use at most 128 MiB of HBM per device.

```python
import math
import jax
import jax.numpy as jnp
import numpy as np
from jax import lax

HEADS = 64
NOPE = 128
ROPE = 64
LAT = 512
VDIM = 128
SEQ = 3072
DOCS = 12


def shared_normal(key):
    return jnp.clip(jax.random.normal(key, (SEQ, LAT + ROPE), jnp.float32), -6.0, 6.0)


def draw_latent(key, part):
    base = shared_normal(key)
    drawn = base
    return drawn.astype(jnp.bfloat16)


def draw_queries(key, part):
    key = jax.random.fold_in(key, 23)
    drawn = jnp.clip(jax.random.normal(key, (SEQ, HEADS, NOPE + ROPE), jnp.float32), -4.0, 4.0)
    return drawn.reshape(SEQ, HEADS * (NOPE + ROPE)).astype(jnp.bfloat16)


def levels(rng, shape, cuts, smallest, largest):
    factor_of = 1.0
    for position, blocks in cuts:
        heights = jax.random.uniform(jax.random.fold_in(jax.random.fold_in(rng, 6), position), (blocks,), jnp.float32, smallest / len(cuts), largest / len(cuts))
        factor_of = factor_of * jnp.repeat(jnp.exp(heights), shape[position] // blocks).reshape((-1,) + (1,) * (len(shape) - 1 - position))
    return factor_of


def profile(count, total, limit, skew):
    loads = [(1 << 20) // math.isqrt(standing ** skew) + 1 for standing in range(2, count + 1)]
    surplus, holding = total - limit - (count - 1), [1] * (count - 1)
    while surplus > 0:
        free = [i for i in range(count - 1) if holding[i] < limit]
        mass, budget = sum([loads[i] for i in free]), surplus
        for i in free:
            extra = min(limit - holding[i], max(1, budget * loads[i] // mass), surplus)
            holding[i] = holding[i] + extra
            surplus = surplus - extra
    return np.array([limit] + holding)


def ragged(own_key, number_of, total, limit, slope):
    if number_of == 2:
        one = jax.random.randint(own_key, (), max(1, total - limit), min(limit, total - 1) + 1)
        return jnp.stack([one, total - one])
    tallies = jnp.asarray(profile(number_of, total, limit, slope), jnp.int32)
    couples = (number_of - 1) // 2
    source_of, taker = tallies[1:1 + 2 * couples:2], tallies[2:2 + 2 * couples:2]
    room = jnp.minimum(source_of - 1, limit - taker)
    passed = jax.random.randint(jax.random.fold_in(own_key, 1), (couples,), 0, 1 << 20) % (room + 1)
    tallies = tallies.at[1:1 + 2 * couples:2].set(source_of - passed).at[2:2 + 2 * couples:2].set(taker + passed)
    return tallies[jax.random.permutation(jax.random.fold_in(own_key, 2), number_of)]


def bell_draw(key, dims, spread, reach, pieces=(), kind=jnp.bfloat16):
    entries = jax.random.normal(key, dims, jnp.float32) * spread
    if len(pieces) > 0:
        entries = levels(key, dims, pieces, -0.22, 0.18) * entries
    return jnp.clip(entries, min=-reach, max=reach).astype(kind)


def setup_inputs(seed: int = 0, part: int = 0) -> dict:
    key_of = jax.random.split(jax.random.key(seed), 6)
    part_splits = jax.random.split(jax.random.fold_in(key_of[5], part), 6)
    return {
        "queries": draw_queries(jax.random.fold_in(jax.random.fold_in(key_of[5], part), 71), part),
        "latent": draw_latent(jax.random.fold_in(jax.random.fold_in(key_of[5], part), 71), part),
        "segments": jnp.searchsorted(jnp.cumsum(ragged(part_splits[2], DOCS, SEQ, SEQ // 2, 2)), jnp.arange(SEQ), side="right").astype(jnp.int32),
        "w_uk": bell_draw(key_of[3], (HEADS, NOPE, LAT), NOPE ** -0.5, 0.5, ((0, 4),)),
        "w_uv": bell_draw(key_of[4], (HEADS, LAT, VDIM), LAT ** -0.5, 0.25, ((0, 4),)),
    }


def reference(queries, latent, segments, w_uk, w_uv):
    shaped = jnp.transpose(queries.reshape(SEQ, HEADS, NOPE + ROPE), (1, 0, 2))
    places = jnp.arange(SEQ, dtype=jnp.int32)
    allowed = (places[None, :] <= places[:, None]) & (segments[None, :] == segments[:, None])
    factor = (NOPE + ROPE) ** -0.5
    values = latent[:, :LAT]

    def one_head(items):
        query_head, key_proj, value_proj = items
        q_lat = jnp.dot(query_head[:, :NOPE], key_proj, preferred_element_type=jnp.float32).astype(jnp.bfloat16)
        joined = jnp.concatenate([q_lat, query_head[:, NOPE:]], axis=1)
        score = jnp.dot(joined, latent.T, preferred_element_type=jnp.float32) * factor
        top = jnp.max(jnp.where(allowed, score, -1e30), axis=1, keepdims=True)
        weights = jnp.where(allowed, jnp.exp(score - top), 0.0)
        total = jnp.sum(weights, axis=1, keepdims=True)
        o_lat = (jnp.dot(weights.astype(jnp.bfloat16), values, preferred_element_type=jnp.float32) / total).astype(jnp.bfloat16)
        return jnp.dot(o_lat, value_proj, preferred_element_type=jnp.float32).astype(jnp.bfloat16)

    result = lax.map(one_head, (shaped, w_uk, w_uv))
    return jnp.transpose(result, (1, 0, 2)).reshape(SEQ, HEADS * VDIM)
```

```python
import functools
import math

import jax
import jax.numpy as jnp
from jax import lax
from jax.experimental import pallas as pl
from jax.experimental.pallas import tpu as pltpu
from jax.sharding import PartitionSpec as P

NOPE = 128
ROPE = 64
LAT = 512
VDIM = 128
LONGEST = 1536
SCALE = math.log2(math.e) / math.sqrt(NOPE + ROPE)
FAR = -1e30
TILE = 256

NT = (((1,), (1,)), ((), ()))


def attention_kernel(
    count_ref, q_ref, lat_ref, keydoc_ref, querydoc_ref, uk_ref, uv_ref, out_ref,
    tail_ref, score_ref, value_ref, top_ref, sum_ref, qcat_ref,
):
    step = pl.program_id(0)
    pairs = pl.num_programs(0) - 1
    rows = q_ref.shape[0]
    count = count_ref[0]
    now = lax.rem(step, 2)
    before = 1 - now
    f32, bf16 = jnp.float32, jnp.bfloat16

    @pl.when(step == 0)
    def _():
        rope = lat_ref[:, LAT : LAT + ROPE].astype(f32) * SCALE
        doc = keydoc_ref[...]
        lane = lax.broadcasted_iota(jnp.int32, (rope.shape[0], ROPE), 1)
        other = jnp.where(doc == lane, 0.0, FAR).astype(f32)
        tail_ref[0] = jnp.concatenate([rope, other], axis=1).astype(bf16)
        tail_ref[1] = jnp.concatenate([other, rope], axis=1).astype(bf16)

    def project(first, size, causal, wide_uk, wide_uv):
        piece = lat_ref[pl.ds(first, size), :LAT]
        keys = lax.dot_general(piece, wide_uk, NT, preferred_element_type=f32)
        keys = (keys * SCALE).astype(bf16)
        values = jnp.dot(piece, wide_uv, preferred_element_type=f32)
        value_ref[now, pl.ds(first, size), :] = values.astype(bf16)
        for head in range(2):
            joined = jnp.concatenate(
                [keys[:, head * 128 : head * 128 + 128], tail_ref[head, pl.ds(first, size), :]],
                axis=1,
            )
            score = lax.dot_general(qcat_ref[head], joined, NT, preferred_element_type=f32)
            if causal:
                row = lax.broadcasted_iota(jnp.int32, score.shape, 0)
                col = lax.broadcasted_iota(jnp.int32, score.shape, 1)
                score = jnp.where(col <= row, score, FAR)
            best = score[:, :128]
            for part in range(1, size // 128):
                best = jnp.maximum(best, score[:, part * 128 : part * 128 + 128])
            if causal:
                top_ref[now, head] = best
            else:
                top_ref[now, head] = jnp.maximum(top_ref[now, head], best)
            for part in range(size // 128):
                score_ref[now, head, first // 128 + part] = score[:, part * 128 : part * 128 + 128]

    def weigh(first, size, causal):
        ones = jnp.ones((size, 128), bf16)
        for head in range(2):
            top = top_ref[before, head]
            weights = jnp.concatenate(
                [
                    jnp.exp2(score_ref[before, head, first // 128 + part] - top).astype(bf16)
                    for part in range(size // 128)
                ],
                axis=1,
            )
            values = value_ref[before, pl.ds(first, size), head * 128 : head * 128 + 128]
            wide = jnp.concatenate([values, ones], axis=1)
            sums = jnp.dot(weights, wide, preferred_element_type=f32)
            if causal:
                sum_ref[head] = sums
            else:
                sum_ref[head] = sum_ref[head] + sums

    def work(projecting, weighing):
        if projecting:
            lane = lax.broadcasted_iota(jnp.int32, (rows, 128), 1)
            low = lane < 64
            left, mid, right = q_ref[:, :128], q_ref[:, 128:256], q_ref[:, 256:384]
            doc = querydoc_ref[...]
            mine = jnp.where(doc == (lane & 63), 1.0, 0.0).astype(bf16)
            qcat_ref[0] = jnp.concatenate([left, jnp.where(low, mid, mine)], axis=1)
            qcat_ref[1] = jnp.concatenate(
                [jnp.where(low, right, mid), jnp.where(low, mine, right)], axis=1
            )
            wide_uk = jnp.concatenate([uk_ref[0], uk_ref[1, 64:], uk_ref[1, :64]], axis=0)
            wide_uv = jnp.concatenate([uv_ref[0], uv_ref[1]], axis=1)
            project(LONGEST, rows, True, wide_uk, wide_uv)
        if weighing:
            weigh(LONGEST, rows, True)

        def body(turn, carry):
            first = pl.multiple_of(LONGEST - (turn + 1) * TILE, TILE)
            if projecting:
                project(first, TILE, False, wide_uk, wide_uv)
            if weighing:
                weigh(first, TILE, False)
            return carry

        lax.fori_loop(0, count, body, 0)
        if projecting:
            for head in range(2):
                best = jnp.max(top_ref[now, head], axis=1, keepdims=True)
                top_ref[now, head] = jnp.broadcast_to(best, (rows, 128))
        if weighing:
            for head in range(2):
                sums = sum_ref[head]
                out_ref[:, head * 128 : head * 128 + 128] = (
                    sums[:, :128] / sums[:, 128:]
                ).astype(bf16)

    @pl.when(step == 0)
    def _():
        work(True, False)

    @pl.when((step > 0) & (step < pairs))
    def _():
        work(True, True)

    @pl.when(step == pairs)
    def _():
        work(False, True)


def attention(count, queries, lat, keydoc, querydoc, w_uk, w_uv):
    rows = queries.shape[0]
    heads = w_uk.shape[0]
    span = lat.shape[0]
    pairs = heads // 2
    last = pairs - 1
    whole = lambda shape: pl.BlockSpec(shape, lambda i, n: (0,) * len(shape))
    return pl.pallas_call(
        attention_kernel,
        grid_spec=pltpu.PrefetchScalarGridSpec(
            num_scalar_prefetch=1,
            grid=(pairs + 1,),
            in_specs=[
                pl.BlockSpec((rows, 2 * (NOPE + ROPE)), lambda i, n: (0, jnp.minimum(i, last))),
                whole(lat.shape),
                whole(keydoc.shape),
                whole(querydoc.shape),
                pl.BlockSpec((2, NOPE, LAT), lambda i, n: (jnp.minimum(i, last), 0, 0)),
                pl.BlockSpec((2, LAT, VDIM), lambda i, n: (jnp.minimum(i, last), 0, 0)),
            ],
            out_specs=pl.BlockSpec((rows, 2 * VDIM), lambda i, n: (0, jnp.maximum(i - 1, 0))),
            scratch_shapes=[
                pltpu.VMEM((2, span, 128), jnp.bfloat16),
                pltpu.VMEM((2, 2, span // 128, rows, 128), jnp.float32),
                pltpu.VMEM((2, span, 256), jnp.bfloat16),
                pltpu.VMEM((2, 2, rows, 128), jnp.float32),
                pltpu.VMEM((2, rows, 256), jnp.float32),
                pltpu.VMEM((2, rows, 256), jnp.bfloat16),
            ],
        ),
        out_shape=jax.ShapeDtypeStruct((rows, heads * VDIM), jnp.bfloat16),
        compiler_params=pltpu.CompilerParams(vmem_limit_bytes=48 << 20),
        name="latent_attention",
    )(count, queries, lat, keydoc, querydoc, w_uk, w_uv)


def shifted(x, by):
    size = lax.axis_size("ctx")
    return lax.ppermute(x, "ctx", [(i, i + by) for i in range(size - by)])


def on_device(queries, latent, segments, w_uk, w_uv):
    rows = queries.shape[0]
    owner = lax.axis_index("ctx")
    mine = lax.all_gather(latent, "head", tiled=True)
    lat = jnp.concatenate([shifted(mine, 4), shifted(mine, 3), shifted(mine, 2), shifted(mine, 1), mine])
    span = lat.shape[0]
    padded = jnp.concatenate([jnp.full((LONGEST,), -1, jnp.int32), segments])
    docs = lax.dynamic_slice(padded, (owner * rows,), (span,))
    earlier = jnp.sum((docs[:LONGEST] == docs[LONGEST]).astype(jnp.int32))
    count = (earlier + TILE - 1) // TILE
    return attention(
        count.reshape(1), queries, lat, docs[:, None], docs[LONGEST:, None], w_uk, w_uv
    )


def solution(mesh):
    placed = (
        P(("dp", "ctx"), "head"),
        P(("dp", "ctx", "head"), None),
        P("dp"),
        P("head", None, None),
        P("head", None, None),
    )
    return jax.shard_map(
        on_device, mesh=mesh, in_specs=placed, out_specs=P(("dp", "ctx"), "head"), check_vma=False
    )
```

```python
import math

import jax
import jax.numpy as jnp
from jax import lax
from jax.experimental import pallas as pl
from jax.experimental.pallas import tpu as pltpu
from jax.sharding import PartitionSpec as P

NOPE = 128
ROPE = 64
LAT = 512
VDIM = 128
SCALE = math.log2(math.e) / math.sqrt(NOPE + ROPE)
FAR = -1e30
TILE = 256
NT = (((1,), (1,)), ((), ()))
f32, bf16 = jnp.float32, jnp.bfloat16


def attention_kernel(
    plan_ref, starts_ref, ends_ref, own_q, mate_q, mine_0, mine_1, mine_2, mine_3, mate_mine,
    older_0, older_1, older_2, older_3, mate_older, uk_ref, uv_ref, out_ref, send_ref,
    lat_ref, tail_ref, score_ref, value_ref, top_ref, sum_ref, qcat_ref,
):
    step = pl.program_id(0)
    pairs = pl.num_programs(0) - 1
    half = own_q.shape[0]
    rows = 2 * half
    past = 2 * rows
    count, wide, core, column = plan_ref[0], plan_ref[1], plan_ref[2], plan_ref[3]
    now = lax.rem(step, 2)
    before = 1 - now

    @pl.when(step == 0)
    def _():
        piece = mine_0.shape[0]

        def place(block, kind, ring, rows_of):
            slot = lax.rem(column + ring, 4)
            first = block * rows + kind * half + slot * piece
            lat_ref[pl.ds(pl.multiple_of(first, 16), piece), :] = rows_of

        other = 1 - core
        rings = (0, 3, 1, 2)
        for k, ref in enumerate((mine_0, mine_1, mine_2, mine_3)):
            place(2, core, rings[k], ref[...])
            place(2, other, rings[k], mate_mine[k * piece : (k + 1) * piece])
        for k, ref in enumerate((older_0, older_1, older_2, older_3)):
            for block in range(2):
                low = block * piece
                place(block, core, rings[k], ref[low : low + piece])
                low = (2 * k + block) * piece
                place(block, other, rings[k], mate_older[low : low + piece])
        keys = lat_ref.shape[0]
        rope = lat_ref[:, LAT:].astype(f32) * SCALE
        at = lax.broadcasted_iota(jnp.int32, (keys, ROPE), 0)
        inside = (at >= starts_ref[:1, :ROPE]) & (at < ends_ref[:1, :ROPE])
        far = jnp.where(inside, 0.0, FAR).astype(f32)
        tail_ref[0] = jnp.concatenate([rope, far], axis=1).astype(bf16)
        tail_ref[1] = jnp.concatenate([far, rope], axis=1).astype(bf16)

    def scores(head, first, size, keys, low, high):
        joined = jnp.concatenate(
            [keys[:, head * 128 : head * 128 + 128], tail_ref[head, pl.ds(first, size), :]], axis=1
        )
        return lax.dot_general(qcat_ref[head, low:high], joined, NT, preferred_element_type=f32)

    def keep(head, first, low, high, score, fresh):
        best = jnp.maximum(score[:, :128], score[:, 128:])
        if fresh:
            top_ref[now, head, low:high] = best
        else:
            top_ref[now, head, low:high] = jnp.maximum(top_ref[now, head, low:high], best)
        score_ref[now, head, first // 128, low:high] = score[:, :128]
        score_ref[now, head, first // 128 + 1, low:high] = score[:, 128:]

    def project(first, size, wide_uk, wide_uv):
        piece = lat_ref[pl.ds(first, size), :LAT]
        keys = lax.dot_general(piece, wide_uk, NT, preferred_element_type=f32)
        values = jnp.dot(piece, wide_uv, preferred_element_type=f32)
        value_ref[now, pl.ds(first, size), :] = values.astype(bf16)
        return (keys * SCALE).astype(bf16)

    def weigh(first, low, high, fresh):
        ones = jnp.ones((TILE, 128), bf16)
        for head in range(2):
            top = top_ref[before, head, low:high]
            weights = jnp.concatenate(
                [
                    jnp.exp2(score_ref[before, head, first // 128 + k, low:high] - top).astype(bf16)
                    for k in range(TILE // 128)
                ],
                axis=1,
            )
            values = value_ref[before, pl.ds(first, TILE), head * 128 : head * 128 + 128]
            sums = jnp.dot(
                weights, jnp.concatenate([values, ones], axis=1), preferred_element_type=f32
            )
            if fresh:
                sum_ref[head, low:high] = sums
            else:
                sum_ref[head, low:high] = sum_ref[head, low:high] + sums

    def work(projecting, weighing):
        if projecting:
            lane = lax.broadcasted_iota(jnp.int32, (rows, 128), 1)
            small = lane < 64
            at = lax.broadcasted_iota(jnp.int32, (rows, 128), 0) + past
            inside = (at >= starts_ref[:1]) & (at < ends_ref[:1])
            doc = jnp.where(inside, 1.0, 0.0).astype(bf16)
            own, mate = own_q[...], mate_q[...]
            lead = core == 0
            whole = jnp.concatenate(
                [jnp.where(lead, own, mate), jnp.where(lead, mate, own)], axis=0
            )
            left, mid, right = whole[:, :128], whole[:, 128:256], whole[:, 256:]
            qcat_ref[0] = jnp.concatenate([left, jnp.where(small, mid, doc)], axis=1)
            qcat_ref[1] = jnp.concatenate(
                [jnp.where(small, right, mid), jnp.where(small, doc, right)], axis=1
            )
            wide_uk = jnp.concatenate([uk_ref[0], uk_ref[1, 64:], uk_ref[1, :64]], axis=0)
            wide_uv = jnp.concatenate([uv_ref[0], uv_ref[1]], axis=1)
        for k in range(rows // TILE):
            first = past + k * TILE
            low = k * TILE
            if projecting:
                keys = project(first, TILE, wide_uk, wide_uv)
                for head in range(2):
                    score = scores(head, first, TILE, keys, low, rows)
                    row = lax.broadcasted_iota(jnp.int32, (TILE, TILE), 0)
                    col = lax.broadcasted_iota(jnp.int32, (TILE, TILE), 1)
                    edge = jnp.where(col <= row, score[:TILE], FAR)
                    if low + TILE < rows:
                        edge = jnp.concatenate([edge, score[TILE:]], axis=0)
                    keep(head, first, low, rows, edge, k == 0)
            if weighing:
                weigh(first, low, rows, k == 0)

        def earlier(high):
            def body(turn, carry):
                first = pl.multiple_of(past - (turn + 1) * TILE, TILE)
                if projecting:
                    keys = project(first, TILE, wide_uk, wide_uv)
                    for head in range(2):
                        score = scores(head, first, TILE, keys, 0, high)
                        keep(head, first, 0, high, score, False)
                if weighing:
                    weigh(first, 0, high, False)
                return carry

            lax.fori_loop(0, count, body, 0)

        @pl.when(wide == 1)
        def _():
            earlier(rows)

        @pl.when(wide == 0)
        def _():
            earlier(rows - TILE)

        if projecting:
            for head in range(2):
                best = jnp.max(top_ref[now, head], axis=1, keepdims=True)
                top_ref[now, head] = jnp.broadcast_to(best, (rows, 128))
        if weighing:
            for head in range(2):
                sums = sum_ref[head]
                ready = (sums[:, :128] / sums[:, 128:]).astype(bf16)
                at = slice(head * 128, head * 128 + 128)
                out_ref[:, at] = jnp.where(core == 0, ready[:half], ready[half:])
                send_ref[:, at] = jnp.where(core == 0, ready[half:], ready[:half])

    @pl.when(step == 0)
    def _():
        work(True, False)

    @pl.when((step > 0) & (step < pairs))
    def _():
        work(True, True)

    @pl.when(step == pairs)
    def _():
        work(False, True)


def attention(plan, starts, ends, queries, mate_queries, mine, mate_mine, older, mate_older, w_uk, w_uv):
    half = queries.shape[0]
    rows = 2 * half
    span = 3 * rows
    heads = w_uk.shape[0]
    pairs = heads // 4
    last = pairs - 1
    whole = lambda x: pl.BlockSpec(x.shape, lambda i, n: (0,) * x.ndim)
    pair = lambda i, n: n[2] * pairs + jnp.minimum(i, last)
    done = lambda i: jnp.maximum(i - 1, 0)
    query = pl.BlockSpec((half, 2 * (NOPE + ROPE)), lambda i, n: (0, pair(i, n)))
    return pl.pallas_call(
        attention_kernel,
        grid_spec=pltpu.PrefetchScalarGridSpec(
            num_scalar_prefetch=1,
            grid=(pairs + 1,),
            in_specs=[
                whole(starts),
                whole(ends),
                query,
                query,
                *[whole(x) for x in mine],
                whole(mate_mine),
                *[whole(x) for x in older],
                whole(mate_older),
                pl.BlockSpec((2, NOPE, LAT), lambda i, n: (pair(i, n), 0, 0)),
                pl.BlockSpec((2, LAT, VDIM), lambda i, n: (pair(i, n), 0, 0)),
            ],
            out_specs=[
                pl.BlockSpec((half, 2 * VDIM), lambda i, n: (0, n[2] * pairs + done(i))),
                pl.BlockSpec((half, 2 * VDIM), lambda i, n: (0, done(i))),
            ],
            scratch_shapes=[
                pltpu.VMEM((span, LAT + ROPE), bf16),
                pltpu.VMEM((2, span, 128), bf16),
                pltpu.VMEM((2, 2, span // 128, rows, 128), f32),
                pltpu.VMEM((2, span, 256), bf16),
                pltpu.VMEM((2, 2, rows, 128), f32),
                pltpu.VMEM((2, rows, 256), f32),
                pltpu.VMEM((2, rows, 256), bf16),
            ],
        ),
        out_shape=[
            jax.ShapeDtypeStruct((half, heads * VDIM), bf16),
            jax.ShapeDtypeStruct((half, heads * VDIM // 2), bf16),
        ],
        compiler_params=pltpu.CompilerParams(vmem_limit_bytes=56 << 20),
        name="latent_attention",
    )(plan, starts, ends, queries, mate_queries, *mine, mate_mine, *older, mate_older, w_uk, w_uv)


def swapped(x):
    size = lax.axis_size("ctx")
    return lax.ppermute(x, "ctx", [(i, i ^ 1) for i in range(size)])


def later(x, chips):
    size = lax.axis_size("ctx")
    return lax.ppermute(x, "ctx", [(i, i + 2 * chips) for i in range(size - 2 * chips)])


def around(x, by):
    size = lax.axis_size("head")
    return lax.ppermute(x, "head", [(i, (i + by) % size) for i in range(size)])


def everywhere(x):
    return [x, around(x, 1), around(x, -1), around(x, 2)]


def on_device(queries, latent, segments, w_uk, w_uv):
    half = queries.shape[0]
    rows = 2 * half
    owner = lax.axis_index("ctx")
    core = lax.rem(owner, 2)
    opening = (owner - core) * half
    bounds = jnp.sum(
        (segments[None, :] < jnp.arange(65, dtype=jnp.int32)[:, None]).astype(jnp.int32), axis=1
    ) - (opening - 2 * rows)
    starts = jnp.tile(bounds[:64], 2)[None]
    ends = jnp.tile(bounds[1:], 2)[None]
    at = 2 * rows
    begin = jnp.max(jnp.where(bounds <= at, bounds, -(1 << 20)))
    finish = jnp.min(jnp.where(bounds > at, bounds, 1 << 20))
    count = (at - begin + TILE - 1) // TILE
    wide = (finish - at > rows - TILE).astype(jnp.int32)
    plan = jnp.stack([count, wide, core, lax.axis_index("head")])

    mate_queries = swapped(queries)
    older = everywhere(jnp.concatenate([later(latent, 2), later(latent, 1)]))
    mine = everywhere(latent)
    mate_mine = swapped(jnp.concatenate(mine))
    mate_older = swapped(jnp.concatenate(older))
    own, send = attention(
        plan, starts, ends, queries, mate_queries, mine, mate_mine, older, mate_older, w_uk, w_uv
    )
    columns = send.shape[1]
    return lax.dynamic_update_slice(own, swapped(send), (0, (1 - core) * columns))


def solution(mesh):
    placed = (
        P(("dp", "ctx"), "head"),
        P(("dp", "ctx", "head"), None),
        P("dp"),
        P("head", None, None),
        P("head", None, None),
    )
    return jax.shard_map(
        on_device, mesh=mesh, in_specs=placed, out_specs=P(("dp", "ctx"), "head"), check_vma=False
    )
```

```python
import math

import jax
import jax.numpy as jnp
from jax import lax
from jax.experimental import pallas as pl
from jax.experimental.pallas import tpu as pltpu
from jax.sharding import PartitionSpec as P

NOPE = 128
ROPE = 64
LAT = 512
VDIM = 128
SCALE = math.log2(math.e) / math.sqrt(NOPE + ROPE)
FAR = -1e30
TILE = 256
WIDE = 512
NT = (((1,), (1,)), ((), ()))
f32, bf16 = jnp.float32, jnp.bfloat16


def attention_kernel(
    plan_ref, starts_ref, ends_ref, own_q, mate_q, mine_0, mine_1, mine_2, mine_3,
    mate_0, mate_1, mate_2, mate_3, uk_ref, uv_ref, out_ref, send_ref,
    lat_ref, tail_ref, score_ref, value_ref, top_ref, total_ref, sum_ref, qcat_ref,
):
    step = pl.program_id(0)
    pairs = pl.num_programs(0) - 1
    half = own_q.shape[0]
    rows = 2 * half
    past = 2 * rows
    count, wide, core, column = plan_ref[0], plan_ref[1], plan_ref[2], plan_ref[3]
    now = lax.rem(step, 2)
    before = 1 - now

    @pl.when(step == 0)
    def _():
        piece = mine_0.shape[0] // 3
        for kind, refs in ((core, (mine_0, mine_1, mine_2, mine_3)), (1 - core, (mate_0, mate_1, mate_2, mate_3))):
            for ring, ref in zip((0, 3, 1, 2), refs):
                slot = lax.rem(column + ring, 4)
                for block in range(3):
                    first = pl.multiple_of(block * rows + kind * half + slot * piece, 16)
                    lat_ref[pl.ds(first, piece), :] = ref[block * piece : (block + 1) * piece]
        keys = lat_ref.shape[0]
        rope = lat_ref[:, LAT:].astype(f32) * SCALE
        at = lax.broadcasted_iota(jnp.int32, (keys, ROPE), 0)
        inside = (at >= starts_ref[:1, :ROPE]) & (at < ends_ref[:1, :ROPE])
        far = jnp.where(inside, 0.0, FAR).astype(f32)
        tail_ref[0] = jnp.concatenate([rope, far], axis=1).astype(bf16)
        tail_ref[1] = jnp.concatenate([far, rope], axis=1).astype(bf16)

    def scores(head, first, size, keys, low, high):
        joined = jnp.concatenate(
            [keys[:, head * 128 : head * 128 + 128], tail_ref[head, pl.ds(first, size), :]], axis=1
        )
        return lax.dot_general(qcat_ref[head, low:high], joined, NT, preferred_element_type=f32)

    def keep(head, first, low, high, score, fresh):
        parts = [score[:, k : k + 128] for k in range(0, score.shape[1], 128)]
        best = parts[0]
        for part in parts[1:]:
            best = jnp.maximum(best, part)
        if not fresh:
            best = jnp.maximum(top_ref[now, head, low:high], best)
        top_ref[now, head, low:high] = best
        for k, part in enumerate(parts):
            score_ref[now, head, first // 128 + k, low:high] = part

    def project(first, size, wide_uk, wide_uv):
        piece = lat_ref[pl.ds(first, size), :LAT]
        keys = lax.dot_general(piece, wide_uk, NT, preferred_element_type=f32)
        values = jnp.dot(piece, wide_uv, preferred_element_type=f32)
        value_ref[now, pl.ds(first, size), :] = values.astype(bf16)
        return (keys * SCALE).astype(bf16)

    def weigh(first, size, low, high, fresh):
        for head in range(2):
            top = top_ref[before, head, low:high]
            weights = [
                jnp.exp2(score_ref[before, head, first // 128 + k, low:high] - top)
                for k in range(size // 128)
            ]
            total = sum(weights[1:], weights[0])
            sums = jnp.dot(
                jnp.concatenate([x.astype(bf16) for x in weights], axis=1),
                value_ref[before, pl.ds(first, size), head * 128 : head * 128 + 128],
                preferred_element_type=f32,
            )
            if not fresh:
                total = total_ref[head, low:high] + total
                sums = sum_ref[head, low:high] + sums
            total_ref[head, low:high] = total
            sum_ref[head, low:high] = sums

    def work(projecting, weighing):
        if projecting:
            lane = lax.broadcasted_iota(jnp.int32, (rows, 128), 1)
            small = lane < 64
            at = lax.broadcasted_iota(jnp.int32, (rows, 128), 0) + past
            inside = (at >= starts_ref[:1]) & (at < ends_ref[:1])
            doc = jnp.where(inside, 1.0, 0.0).astype(bf16)
            own, mate = own_q[...], mate_q[...]
            lead = core == 0
            whole = jnp.concatenate(
                [jnp.where(lead, own, mate), jnp.where(lead, mate, own)], axis=0
            )
            left, mid, right = whole[:, :128], whole[:, 128:256], whole[:, 256:]
            qcat_ref[0] = jnp.concatenate([left, jnp.where(small, mid, doc)], axis=1)
            qcat_ref[1] = jnp.concatenate(
                [jnp.where(small, right, mid), jnp.where(small, doc, right)], axis=1
            )
            wide_uk = jnp.concatenate([uk_ref[0], uk_ref[1, 64:], uk_ref[1, :64]], axis=0)
            wide_uv = jnp.concatenate([uv_ref[0], uv_ref[1]], axis=1)
        for k in range(rows // TILE):
            first = past + k * TILE
            low = k * TILE
            if projecting:
                keys = project(first, TILE, wide_uk, wide_uv)
                for head in range(2):
                    score = scores(head, first, TILE, keys, low, rows)
                    row = lax.broadcasted_iota(jnp.int32, (TILE, TILE), 0)
                    col = lax.broadcasted_iota(jnp.int32, (TILE, TILE), 1)
                    edge = jnp.where(col <= row, score[:TILE], FAR)
                    if low + TILE < rows:
                        edge = jnp.concatenate([edge, score[TILE:]], axis=0)
                    keep(head, first, low, rows, edge, k == 0)
            if weighing:
                weigh(first, TILE, low, rows, k == 0)

        def earlier(high):
            def body(turn, carry):
                first = pl.multiple_of(past - (turn + 1) * WIDE, WIDE)
                if projecting:
                    keys = project(first, WIDE, wide_uk, wide_uv)
                    for head in range(2):
                        score = scores(head, first, WIDE, keys, 0, high)
                        keep(head, first, 0, high, score, False)
                if weighing:
                    weigh(first, WIDE, 0, high, False)
                return carry

            lax.fori_loop(0, count, body, 0)

        @pl.when(wide == 1)
        def _():
            earlier(rows)

        @pl.when(wide == 0)
        def _():
            earlier(rows - TILE)

        if projecting:
            for head in range(2):
                best = jnp.max(top_ref[now, head], axis=1, keepdims=True)
                top_ref[now, head] = jnp.broadcast_to(best, (rows, 128))
        if weighing:
            for head in range(2):
                total = jnp.sum(total_ref[head], axis=1, keepdims=True)
                ready = (sum_ref[head] * (1.0 / total)).astype(bf16)
                at = slice(head * 128, head * 128 + 128)
                out_ref[:, at] = jnp.where(core == 0, ready[:half], ready[half:])
                send_ref[:, at] = jnp.where(core == 0, ready[half:], ready[:half])

    @pl.when(step == 0)
    def _():
        work(True, False)

    @pl.when((step > 0) & (step < pairs))
    def _():
        work(True, True)

    @pl.when(step == pairs)
    def _():
        work(False, True)


def attention(plan, starts, ends, queries, mate_queries, mine, mate, w_uk, w_uv):
    half = queries.shape[0]
    rows = 2 * half
    span = 3 * rows
    heads = w_uk.shape[0]
    pairs = heads // 4
    last = pairs - 1
    whole = lambda x: pl.BlockSpec(x.shape, lambda i, n: (0,) * x.ndim)
    pair = lambda i, n: n[2] * pairs + jnp.minimum(i, last)
    done = lambda i: jnp.maximum(i - 1, 0)
    query = pl.BlockSpec((half, 2 * (NOPE + ROPE)), lambda i, n: (0, pair(i, n)))
    return pl.pallas_call(
        attention_kernel,
        grid_spec=pltpu.PrefetchScalarGridSpec(
            num_scalar_prefetch=1,
            grid=(pairs + 1,),
            in_specs=[
                whole(starts),
                whole(ends),
                query,
                query,
                *[whole(x) for x in mine],
                *[whole(x) for x in mate],
                pl.BlockSpec((2, NOPE, LAT), lambda i, n: (pair(i, n), 0, 0)),
                pl.BlockSpec((2, LAT, VDIM), lambda i, n: (pair(i, n), 0, 0)),
            ],
            out_specs=[
                pl.BlockSpec((half, 2 * VDIM), lambda i, n: (0, n[2] * pairs + done(i))),
                pl.BlockSpec((half, 2 * VDIM), lambda i, n: (0, done(i))),
            ],
            scratch_shapes=[
                pltpu.VMEM((span, LAT + ROPE), bf16),
                pltpu.VMEM((2, span, 128), bf16),
                pltpu.VMEM((2, 2, span // 128, rows, 128), f32),
                pltpu.VMEM((2, span, 256), bf16),
                pltpu.VMEM((2, 2, rows, 128), f32),
                pltpu.VMEM((2, rows, 128), f32),
                pltpu.VMEM((2, rows, 128), f32),
                pltpu.VMEM((2, rows, 256), bf16),
            ],
        ),
        out_shape=[
            jax.ShapeDtypeStruct((half, heads * VDIM), bf16),
            jax.ShapeDtypeStruct((half, heads * VDIM // 2), bf16),
        ],
        compiler_params=pltpu.CompilerParams(vmem_limit_bytes=56 << 20),
        name="latent_attention",
    )(plan, starts, ends, queries, mate_queries, *mine, *mate, w_uk, w_uv)


def swapped(x):
    size = lax.axis_size("ctx")
    return lax.ppermute(x, "ctx", [(i, i ^ 1) for i in range(size)])


def later(x, chips):
    size = lax.axis_size("ctx")
    return lax.ppermute(x, "ctx", [(i, i + 2 * chips) for i in range(size - 2 * chips)])


def around(x, by):
    size = lax.axis_size("head")
    return lax.ppermute(x, "head", [(i, (i + by) % size) for i in range(size)])


def everywhere(x):
    return [x, around(x, 1), around(x, -1), around(x, 2)]


def on_device(queries, latent, segments, w_uk, w_uv):
    half = queries.shape[0]
    rows = 2 * half
    owner = lax.axis_index("ctx")
    core = lax.rem(owner, 2)
    opening = (owner - core) * half
    bounds = jnp.sum(
        (segments[None, :] < jnp.arange(65, dtype=jnp.int32)[:, None]).astype(jnp.int32), axis=1
    ) - (opening - 2 * rows)
    starts = jnp.tile(bounds[:64], 2)[None]
    ends = jnp.tile(bounds[1:], 2)[None]
    at = 2 * rows
    begin = jnp.max(jnp.where(bounds <= at, bounds, -(1 << 20)))
    finish = jnp.min(jnp.where(bounds > at, bounds, 1 << 20))
    count = (at - begin + WIDE - 1) // WIDE
    wide = (finish - at > rows - TILE).astype(jnp.int32)
    plan = jnp.stack([count, wide, core, lax.axis_index("head")])

    piece = jnp.concatenate([later(latent, 2), later(latent, 1), latent])
    piece, plan, starts, ends = lax.optimization_barrier((piece, plan, starts, ends))
    mine = everywhere(piece)
    mate = [swapped(x) for x in mine]
    own, send = attention(
        plan, starts, ends, queries, swapped(queries), mine, mate, w_uk, w_uv
    )
    columns = send.shape[1]
    return lax.dynamic_update_slice(own, swapped(send), (0, (1 - core) * columns))


def solution(mesh):
    placed = (
        P(("dp", "ctx"), "head"),
        P(("dp", "ctx", "head"), None),
        P("dp"),
        P("head", None, None),
        P("head", None, None),
    )
    return jax.shard_map(
        on_device, mesh=mesh, in_specs=placed, out_specs=P(("dp", "ctx"), "head"), check_vma=False
    )
```

```python
import functools
import math

import jax
import jax.numpy as jnp
from jax import lax
from jax.experimental import pallas as pl
from jax.experimental.pallas import tpu as pltpu
from jax.sharding import PartitionSpec as P

NOPE = 128
ROPE = 64
LAT = 512
VDIM = 128
SCALE = math.log2(math.e) / math.sqrt(NOPE + ROPE)
FAR = -1e30
TILE = 256
WIDE = 512
NT = (((1,), (1,)), ((), ()))
f32, bf16 = jnp.float32, jnp.bfloat16


def attention_kernel(diagonal, blocks, *refs):
    plan_ref, edges_ref, own_q, mate_q, uk_ref, uv_ref = refs[:6]
    mine, mate = refs[6:10], refs[10:14]
    refs = refs[14:]
    if diagonal:
        out_sum, out_total, out_top = refs[:3]
        lat_ref, tail_ref, score_ref, value_ref, top_ref, qcat_ref = refs[3:]
    else:
        in_sum, in_total, in_top, next_top, out_ref, send_ref = refs[:6]
        lat_ref, tail_ref, score_ref, value_ref, top_ref, qcat_ref, sum_ref, total_ref, bound_ref = refs[6:]
    step = pl.program_id(0)
    pairs = pl.num_programs(0) - 1
    half = own_q.shape[0]
    rows = 2 * half
    past = 2 * rows
    base = past if diagonal else 0
    core, column = plan_ref[0], plan_ref[1]
    now = lax.rem(step, 2)
    before = 1 - now

    @pl.when(step == 0)
    def _():
        piece = mine[0].shape[0] // blocks
        for kind, group in ((core, mine), (1 - core, mate)):
            for ring, ref in zip((0, 3, 1, 2), group):
                slot = lax.rem(column + ring, 4)
                for block in range(blocks):
                    first = pl.multiple_of(block * rows + kind * half + slot * piece, 16)
                    lat_ref[pl.ds(first, piece), :] = ref[block * piece : (block + 1) * piece]
        keys = lat_ref.shape[0]
        rope = lat_ref[:, LAT:].astype(f32) * SCALE
        at = lax.broadcasted_iota(jnp.int32, (keys, ROPE), 0) + base
        inside = (at >= edges_ref[:1, :ROPE]) & (at < edges_ref[1:, :ROPE])
        far = jnp.where(inside, 0.0, FAR).astype(f32)
        tail_ref[0] = jnp.concatenate([rope, far], axis=1).astype(bf16)
        tail_ref[1] = jnp.concatenate([far, rope], axis=1).astype(bf16)
        if not diagonal:
            lows, highs = edges_ref[:1].astype(f32), edges_ref[1:].astype(f32)
            begin = jnp.max(jnp.where(lows <= past, lows, -1e9)).astype(jnp.int32)
            finish = jnp.min(jnp.where(highs > past, highs, 1e9)).astype(jnp.int32)
            bound_ref[0] = lax.div(past - begin + WIDE - 1, WIDE)
            bound_ref[1] = finish - past

    def scores(head, first, size, keys, low, high):
        joined = jnp.concatenate(
            [keys[:, head * 128 : head * 128 + 128], tail_ref[head, pl.ds(first, size), :]], axis=1
        )
        return lax.dot_general(qcat_ref[head, low:high], joined, NT, preferred_element_type=f32)

    def keep(head, first, low, high, score, fresh):
        parts = [score[:, k : k + 128] for k in range(0, score.shape[1], 128)]
        best = parts[0]
        for part in parts[1:]:
            best = jnp.maximum(best, part)
        if not fresh:
            best = jnp.maximum(top_ref[now, head, low:high], best)
        top_ref[now, head, low:high] = best
        for k, part in enumerate(parts):
            score_ref[now, head, first // 128 + k, low:high] = part

    def project(first, size, wide_uk, wide_uv):
        piece = lat_ref[pl.ds(first, size), :LAT]
        keys = lax.dot_general(piece, wide_uk, NT, preferred_element_type=f32)
        values = jnp.dot(piece, wide_uv, preferred_element_type=f32)
        value_ref[now, pl.ds(first, size), :] = values.astype(bf16)
        return (keys * SCALE).astype(bf16)

    def weigh(head, first, size, low, high):
        top = top_ref[before, head, low:high]
        weights = [
            jnp.exp2(score_ref[before, head, first // 128 + k, low:high] - top)
            for k in range(size // 128)
        ]
        sums = jnp.dot(
            jnp.concatenate([x.astype(bf16) for x in weights], axis=1),
            value_ref[before, pl.ds(first, size), head * 128 : head * 128 + 128],
            preferred_element_type=f32,
        )
        return sums, sum(weights[1:], weights[0])

    def work(projecting, weighing):
        if projecting:
            lane = lax.broadcasted_iota(jnp.int32, (rows, 128), 1)
            small = lane < 64
            at = lax.broadcasted_iota(jnp.int32, (rows, 128), 0) + past
            inside = (at >= edges_ref[:1]) & (at < edges_ref[1:])
            doc = jnp.where(inside, 1.0, 0.0).astype(bf16)
            own, other = own_q[...], mate_q[...]
            lead = core == 0
            whole = jnp.concatenate(
                [jnp.where(lead, own, other), jnp.where(lead, other, own)], axis=0
            )
            left, mid, right = whole[:, :128], whole[:, 128:256], whole[:, 256:]
            qcat_ref[0] = jnp.concatenate([left, jnp.where(small, mid, doc)], axis=1)
            qcat_ref[1] = jnp.concatenate(
                [jnp.where(small, right, mid), jnp.where(small, doc, right)], axis=1
            )
            wide_uk = jnp.concatenate([uk_ref[0], uk_ref[1, 64:], uk_ref[1, :64]], axis=0)
            wide_uv = jnp.concatenate([uv_ref[0], uv_ref[1]], axis=1)
        if diagonal:
            if projecting:
                keys = project(0, rows, wide_uk, wide_uv)
            for low in range(0, rows, TILE):
                for head in range(2):
                    if projecting:
                        score = scores(head, low, TILE, keys[low : low + TILE], low, rows)
                        row = lax.broadcasted_iota(jnp.int32, (TILE, TILE), 0)
                        col = lax.broadcasted_iota(jnp.int32, (TILE, TILE), 1)
                        edge = jnp.where(col <= row, score[:TILE], FAR)
                        if low + TILE < rows:
                            edge = jnp.concatenate([edge, score[TILE:]], axis=0)
                        keep(head, low, low, rows, edge, low == 0)
                    if weighing:
                        high = low + TILE
                        sums, total = weigh(head, 0, high, low, high)
                        out_sum[head, low:high] = sums
                        out_total[head, low:high] = total
                        out_top[head, low:high] = top_ref[before, head, low:high]
        else:
            for head in range(2):
                if projecting:
                    top_ref[now, head] = next_top[head]
                if weighing:
                    scale = jnp.exp2(in_top[head] - top_ref[before, head])
                    sum_ref[head] = in_sum[head] * scale
                    total_ref[head] = in_total[head] * scale

            def earlier(high):
                def body(turn, carry):
                    first = pl.multiple_of(past - (turn + 1) * WIDE, WIDE)
                    if projecting:
                        keys = project(first, WIDE, wide_uk, wide_uv)
                    for head in range(2):
                        if projecting:
                            score = scores(head, first, WIDE, keys, 0, high)
                            keep(head, first, 0, high, score, False)
                        if weighing:
                            sums, total = weigh(head, first, WIDE, 0, high)
                            sum_ref[head, :high] = sum_ref[head, :high] + sums
                            total_ref[head, :high] = total_ref[head, :high] + total
                    return carry

                lax.fori_loop(0, bound_ref[0], body, 0)

            reach = bound_ref[1]
            for high in range(TILE, rows + 1, TILE):
                fits = reach > high - TILE
                if high < rows:
                    fits = fits & (reach <= high)
                pl.when(fits)(functools.partial(earlier, high))

        if projecting:
            for head in range(2):
                best = jnp.max(top_ref[now, head], axis=1, keepdims=True)
                top_ref[now, head] = jnp.broadcast_to(best, (rows, 128))
        if weighing and not diagonal:
            for head in range(2):
                total = jnp.sum(total_ref[head], axis=1, keepdims=True)
                ready = (sum_ref[head] * (1.0 / total)).astype(bf16)
                at = slice(head * 128, head * 128 + 128)
                out_ref[:, at] = jnp.where(core == 0, ready[:half], ready[half:])
                send_ref[:, at] = jnp.where(core == 0, ready[half:], ready[:half])

    @pl.when(step == 0)
    def _():
        work(True, False)

    @pl.when((step > 0) & (step < pairs))
    def _():
        work(True, True)

    @pl.when(step == pairs)
    def _():
        work(False, True)


def attention(plan, edges, queries, mate_queries, w_uk, w_uv, mine, mate, state):
    half = queries.shape[0]
    rows = 2 * half
    heads = w_uk.shape[0]
    pairs = heads // 4
    last = pairs - 1
    diagonal = state is None
    blocks = 1 if diagonal else 2
    span = blocks * rows
    whole = lambda x: pl.BlockSpec(x.shape, lambda i, n: (0,) * x.ndim)
    pair = lambda i, n: n[0] * pairs + jnp.minimum(i, last)
    done = lambda i: jnp.maximum(i - 1, 0)
    query = pl.BlockSpec((half, 2 * (NOPE + ROPE)), lambda i, n: (0, pair(i, n)))
    part = pl.BlockSpec((2, rows, 128), lambda i, n: (done(i), 0, 0))
    coming = pl.BlockSpec((2, rows, 128), lambda i, n: (jnp.minimum(i, last), 0, 0))
    scratch = [
        pltpu.VMEM((span, LAT + ROPE), bf16),
        pltpu.VMEM((2, span, 128), bf16),
        pltpu.VMEM((2, 2, span // 128, rows, 128), f32),
        pltpu.VMEM((2, span, 256), bf16),
        pltpu.VMEM((2, 2, rows, 128), f32),
        pltpu.VMEM((2, rows, 256), bf16),
    ]
    if diagonal:
        extra, more = [], []
        out_specs = [part] * 3
        out_shape = [jax.ShapeDtypeStruct((heads // 2, rows, 128), f32)] * 3
    else:
        extra, more = [part, part, part, coming], [*state, state[2]]
        scratch += [pltpu.VMEM((2, rows, 128), f32)] * 2 + [pltpu.SMEM((2,), jnp.int32)]
        out_specs = [
            pl.BlockSpec((half, 2 * VDIM), lambda i, n: (0, n[0] * pairs + done(i))),
            pl.BlockSpec((half, 2 * VDIM), lambda i, n: (0, done(i))),
        ]
        out_shape = [
            jax.ShapeDtypeStruct((half, heads * VDIM), bf16),
            jax.ShapeDtypeStruct((half, heads * VDIM // 2), bf16),
        ]
    return pl.pallas_call(
        functools.partial(attention_kernel, diagonal, blocks),
        grid_spec=pltpu.PrefetchScalarGridSpec(
            num_scalar_prefetch=1,
            grid=(pairs + 1,),
            in_specs=[
                whole(edges),
                query,
                query,
                pl.BlockSpec((2, NOPE, LAT), lambda i, n: (pair(i, n), 0, 0)),
                pl.BlockSpec((2, LAT, VDIM), lambda i, n: (pair(i, n), 0, 0)),
                *[whole(x) for x in mine],
                *[whole(x) for x in mate],
                *extra,
            ],
            out_specs=out_specs,
            scratch_shapes=scratch,
        ),
        out_shape=out_shape,
        compiler_params=pltpu.CompilerParams(vmem_limit_bytes=48 << 20),
        cost_estimate=pl.CostEstimate(
            flops=16 << 30, bytes_accessed=16 << 20, transcendentals=rows * span * heads // 2
        ),
        name="diagonal_attention" if diagonal else "earlier_attention",
    )(plan, edges, queries, mate_queries, w_uk, w_uv, *mine, *mate, *more)


def swapped(x):
    size = lax.axis_size("ctx")
    return lax.ppermute(x, "ctx", [(i, i ^ 1) for i in range(size)])


def later(x, chips):
    size = lax.axis_size("ctx")
    return lax.ppermute(x, "ctx", [(i, i + 2 * chips) for i in range(size - 2 * chips)])


def around(x, by):
    size = lax.axis_size("head")
    return lax.ppermute(x, "head", [(i, (i + by) % size) for i in range(size)])


def everywhere(x):
    return [x, around(x, 1), around(x, -1), around(x, 2)]


def on_device(queries, latent, segments, w_uk, w_uv):
    half = queries.shape[0]
    rows = 2 * half
    owner = lax.axis_index("ctx")
    core = lax.rem(owner, 2)
    opening = (owner - core) * half
    label = jnp.arange(128, dtype=jnp.int32) % 64
    label = jnp.stack([label, label + 1])
    edges = jnp.sum((segments[None, None, :] < label[:, :, None]).astype(jnp.int32), axis=2)
    edges = edges - (opening - 2 * rows)
    plan = jnp.stack([core, lax.axis_index("head")])

    mate_queries = swapped(queries)
    older = jnp.concatenate([later(latent, 2), later(latent, 1)])
    mine = everywhere(latent)
    mate = [swapped(x) for x in mine]
    older, plan, edges = lax.optimization_barrier((older, plan, edges))
    older_mine = everywhere(older)
    state = attention(plan, edges, queries, mate_queries, w_uk, w_uv, mine, mate, None)
    older_mate = [swapped(older_mine[0])]
    state, arrived = lax.optimization_barrier((state, older_mine[1:]))
    older_mine = [older_mine[0], *arrived]
    older_mate += [swapped(x) for x in arrived]
    own, send = attention(
        plan, edges, queries, mate_queries, w_uk, w_uv, older_mine, older_mate, state
    )
    columns = send.shape[1]
    return lax.dynamic_update_slice(own, swapped(send), (0, (1 - core) * columns))


def solution(mesh):
    placed = (
        P(("dp", "ctx"), "head"),
        P(("dp", "ctx", "head"), None),
        P("dp"),
        P("head", None, None),
        P("head", None, None),
    )
    return jax.shard_map(
        on_device, mesh=mesh, in_specs=placed, out_specs=P(("dp", "ctx"), "head"), check_vma=False
    )
```

```python
import functools
import math

import jax
import jax.numpy as jnp
from jax import lax
from jax.experimental import pallas as pl
from jax.experimental.pallas import tpu as pltpu
from jax.sharding import PartitionSpec as P

NOPE = 128
ROPE = 64
LAT = 512
VDIM = 128
SCALE = math.log2(math.e) / math.sqrt(NOPE + ROPE)
FAR = -1e30
TILE = 256
WIDE = 512
NT = (((1,), (1,)), ((), ()))
f32, bf16 = jnp.float32, jnp.bfloat16


def attention_kernel(diagonal, blocks, *refs):
    plan_ref, edges_ref, own_q, mate_q, uk_ref, uv_ref = refs[:6]
    mine = refs[6:10]
    if diagonal:
        piece = mine[0].shape[0]
        mate = [refs[10].at[k * piece : (k + 1) * piece] for k in range(4)]
        refs = refs[11:]
    else:
        mate, refs = refs[10:14], refs[14:]
    if diagonal:
        out_mean, out_weight = refs[:2]
        lat_ref, tail_ref, score_ref, value_ref, top_ref, qcat_ref = refs[2:]
    else:
        in_mean, in_weight, out_ref, send_ref = refs[:4]
        lat_ref, tail_ref, score_ref, value_ref, top_ref, qcat_ref = refs[4:10]
        sum_ref, total_ref, weight_ref, bound_ref = refs[10:]
    step = pl.program_id(0)
    pairs = pl.num_programs(0) - 1
    half = own_q.shape[0]
    rows = 2 * half
    past = 2 * rows
    base = past if diagonal else 0
    core, column = plan_ref[0], plan_ref[1]
    now = lax.rem(step, 2)
    before = 1 - now

    @pl.when(step == 0)
    def _():
        piece = mine[0].shape[0] // blocks
        for kind, group in ((core, mine), (1 - core, mate)):
            for ring, ref in zip((0, 3, 1, 2), group):
                slot = lax.rem(column + ring, 4)
                for block in range(blocks):
                    first = pl.multiple_of(block * rows + kind * half + slot * piece, 16)
                    lat_ref[pl.ds(first, piece), :] = ref[block * piece : (block + 1) * piece]
        keys = lat_ref.shape[0]
        rope = lat_ref[:, LAT:].astype(f32) * SCALE
        at = lax.broadcasted_iota(jnp.int32, (keys, ROPE), 0) + base
        inside = (at >= edges_ref[:1, :ROPE]) & (at < edges_ref[1:, :ROPE])
        far = jnp.where(inside, 0.0, FAR).astype(f32)
        tail_ref[0] = jnp.concatenate([rope, far], axis=1).astype(bf16)
        tail_ref[1] = jnp.concatenate([far, rope], axis=1).astype(bf16)
        if not diagonal:
            lows, highs = edges_ref[:1].astype(f32), edges_ref[1:].astype(f32)
            begin = jnp.max(jnp.where(lows <= past, lows, -1e9)).astype(jnp.int32)
            finish = jnp.min(jnp.where(highs > past, highs, 1e9)).astype(jnp.int32)
            bound_ref[0] = lax.div(past - begin + WIDE - 1, WIDE)
            bound_ref[1] = finish - past

    def scores(head, first, size, keys, low, high):
        joined = jnp.concatenate(
            [keys[:, head * 128 : head * 128 + 128], tail_ref[head, pl.ds(first, size), :]], axis=1
        )
        return lax.dot_general(qcat_ref[head, low:high], joined, NT, preferred_element_type=f32)

    def keep(head, first, low, high, score, fresh):
        parts = [score[:, k : k + 128] for k in range(0, score.shape[1], 128)]
        best = parts[0]
        for part in parts[1:]:
            best = jnp.maximum(best, part)
        if not fresh:
            best = jnp.maximum(top_ref[now, head, low:high], best)
        top_ref[now, head, low:high] = best
        for k, part in enumerate(parts):
            score_ref[now, head, first // 128 + k, low:high] = part

    def project(first, size, wide_uk, wide_uv):
        piece = lat_ref[pl.ds(first, size), :LAT]
        keys = lax.dot_general(piece, wide_uk, NT, preferred_element_type=f32)
        values = jnp.dot(piece, wide_uv, preferred_element_type=f32)
        value_ref[now, pl.ds(first, size), :] = values.astype(bf16)
        return (keys * SCALE).astype(bf16)

    def weigh(head, first, size, low, high):
        top = top_ref[before, head, low:high]
        weights = [
            jnp.exp2(score_ref[before, head, first // 128 + k, low:high] - top)
            for k in range(size // 128)
        ]
        sums = jnp.dot(
            jnp.concatenate([x.astype(bf16) for x in weights], axis=1),
            value_ref[before, pl.ds(first, size), head * 128 : head * 128 + 128],
            preferred_element_type=f32,
        )
        return sums, sum(weights[1:], weights[0])

    def work(projecting, weighing):
        if projecting:
            lane = lax.broadcasted_iota(jnp.int32, (rows, 128), 1)
            small = lane < 64
            at = lax.broadcasted_iota(jnp.int32, (rows, 128), 0) + past
            inside = (at >= edges_ref[:1]) & (at < edges_ref[1:])
            doc = jnp.where(inside, 1.0, 0.0).astype(bf16)
            own, other = own_q[...], mate_q[...]
            lead = core == 0
            whole = jnp.concatenate(
                [jnp.where(lead, own, other), jnp.where(lead, other, own)], axis=0
            )
            left, mid, right = whole[:, :128], whole[:, 128:256], whole[:, 256:]
            qcat_ref[0] = jnp.concatenate([left, jnp.where(small, mid, doc)], axis=1)
            qcat_ref[1] = jnp.concatenate(
                [jnp.where(small, right, mid), jnp.where(small, doc, right)], axis=1
            )
            wide_uk = jnp.concatenate([uk_ref[0], uk_ref[1, 64:], uk_ref[1, :64]], axis=0)
            wide_uv = jnp.concatenate([uv_ref[0], uv_ref[1]], axis=1)
        if diagonal:
            if projecting:
                keys = project(0, rows, wide_uk, wide_uv)
            for low in range(0, rows, TILE):
                for head in range(2):
                    if projecting:
                        score = scores(head, low, TILE, keys[low : low + TILE], low, rows)
                        row = lax.broadcasted_iota(jnp.int32, (TILE, TILE), 0)
                        col = lax.broadcasted_iota(jnp.int32, (TILE, TILE), 1)
                        edge = jnp.where(col <= row, score[:TILE], FAR)
                        if low + TILE < rows:
                            edge = jnp.concatenate([edge, score[TILE:]], axis=0)
                        keep(head, low, low, rows, edge, low == 0)
                    if weighing:
                        high = low + TILE
                        sums, total = weigh(head, 0, high, low, high)
                        total = jnp.sum(total, axis=1, keepdims=True)
                        out_mean[head, low:high] = sums * (1.0 / total)
                        out_weight[head, low:high] = top_ref[before, head, low:high] + jnp.log2(total)
        else:
            for head in range(2):
                if projecting:
                    top_ref[now, head] = in_weight[head]
                    weight_ref[now, head] = in_weight[head]
                if weighing:
                    scale = jnp.exp2(weight_ref[before, head] - top_ref[before, head])
                    sum_ref[head] = in_mean[head] * scale
                    total_ref[head] = scale * (1.0 / 128)

            def earlier(high):
                def body(turn, carry):
                    first = pl.multiple_of(past - (turn + 1) * WIDE, WIDE)
                    if projecting:
                        keys = project(first, WIDE, wide_uk, wide_uv)
                    for head in range(2):
                        if projecting:
                            score = scores(head, first, WIDE, keys, 0, high)
                            keep(head, first, 0, high, score, False)
                        if weighing:
                            sums, total = weigh(head, first, WIDE, 0, high)
                            sum_ref[head, :high] = sum_ref[head, :high] + sums
                            total_ref[head, :high] = total_ref[head, :high] + total
                    return carry

                lax.fori_loop(0, bound_ref[0], body, 0)

            reach = bound_ref[1]
            for high in range(TILE, rows + 1, TILE):
                fits = reach > high - TILE
                if high < rows:
                    fits = fits & (reach <= high)
                pl.when(fits)(functools.partial(earlier, high))

        if projecting:
            for head in range(2):
                best = jnp.max(top_ref[now, head], axis=1, keepdims=True)
                top_ref[now, head] = jnp.broadcast_to(best, (rows, 128))
        if weighing and not diagonal:
            for head in range(2):
                total = jnp.sum(total_ref[head], axis=1, keepdims=True)
                ready = (sum_ref[head] * (1.0 / total)).astype(bf16)
                at = slice(head * 128, head * 128 + 128)
                out_ref[:, at] = jnp.where(core == 0, ready[:half], ready[half:])
                send_ref[:, at] = jnp.where(core == 0, ready[half:], ready[:half])

    @pl.when(step == 0)
    def _():
        work(True, False)

    @pl.when((step > 0) & (step < pairs))
    def _():
        work(True, True)

    @pl.when(step == pairs)
    def _():
        work(False, True)


def attention(plan, edges, queries, mate_queries, w_uk, w_uv, mine, mate, state):
    half = queries.shape[0]
    rows = 2 * half
    heads = w_uk.shape[0]
    pairs = heads // 4
    last = pairs - 1
    diagonal = state is None
    blocks = 1 if diagonal else 2
    span = blocks * rows
    whole = lambda x: pl.BlockSpec(x.shape, lambda i, n: (0,) * x.ndim)
    pair = lambda i, n: n[0] * pairs + jnp.minimum(i, last)
    done = lambda i: jnp.maximum(i - 1, 0)
    query = pl.BlockSpec((half, 2 * (NOPE + ROPE)), lambda i, n: (0, pair(i, n)))
    part = pl.BlockSpec((2, rows, 128), lambda i, n: (done(i), 0, 0))
    coming = pl.BlockSpec((2, rows, 128), lambda i, n: (jnp.minimum(i, last), 0, 0))
    scratch = [
        pltpu.VMEM((span, LAT + ROPE), bf16),
        pltpu.VMEM((2, span, 128), bf16),
        pltpu.VMEM((2, 2, span // 128, rows, 128), f32),
        pltpu.VMEM((2, span, 256), bf16),
        pltpu.VMEM((2, 2, rows, 128), f32),
        pltpu.VMEM((2, rows, 256), bf16),
    ]
    if diagonal:
        extra, more = [], []
        out_specs = [part] * 2
        out_shape = [jax.ShapeDtypeStruct((heads // 2, rows, 128), f32)] * 2
    else:
        extra, more = [part, coming], state
        scratch += [pltpu.VMEM((2, rows, 128), f32)] * 2
        scratch += [pltpu.VMEM((2, 2, rows, 128), f32), pltpu.SMEM((2,), jnp.int32)]
        out_specs = [
            pl.BlockSpec((half, 2 * VDIM), lambda i, n: (0, n[0] * pairs + done(i))),
            pl.BlockSpec((half, 2 * VDIM), lambda i, n: (0, done(i))),
        ]
        out_shape = [
            jax.ShapeDtypeStruct((half, heads * VDIM), bf16),
            jax.ShapeDtypeStruct((half, heads * VDIM // 2), bf16),
        ]
    return pl.pallas_call(
        functools.partial(attention_kernel, diagonal, blocks),
        grid_spec=pltpu.PrefetchScalarGridSpec(
            num_scalar_prefetch=1,
            grid=(pairs + 1,),
            in_specs=[
                whole(edges),
                query,
                query,
                pl.BlockSpec((2, NOPE, LAT), lambda i, n: (pair(i, n), 0, 0)),
                pl.BlockSpec((2, LAT, VDIM), lambda i, n: (pair(i, n), 0, 0)),
                *[whole(x) for x in mine],
                *[whole(x) for x in mate],
                *extra,
            ],
            out_specs=out_specs,
            scratch_shapes=scratch,
        ),
        out_shape=out_shape,
        compiler_params=pltpu.CompilerParams(vmem_limit_bytes=60 << 20),
        cost_estimate=pl.CostEstimate(
            flops=16 << 30, bytes_accessed=16 << 20, transcendentals=rows * span * heads // 2
        ),
        name="diagonal_attention" if diagonal else "earlier_attention",
    )(plan, edges, queries, mate_queries, w_uk, w_uv, *mine, *mate, *more)


def swapped(x):
    size = lax.axis_size("ctx")
    return lax.ppermute(x, "ctx", [(i, i ^ 1) for i in range(size)])


def later(x, chips):
    size = lax.axis_size("ctx")
    return lax.ppermute(x, "ctx", [(i, i + 2 * chips) for i in range(size - 2 * chips)])


def around(x, by):
    size = lax.axis_size("head")
    return lax.ppermute(x, "head", [(i, (i + by) % size) for i in range(size)])


def everywhere(x):
    return [x, around(x, 1), around(x, -1), around(x, 2)]


def on_device(queries, latent, segments, w_uk, w_uv):
    half = queries.shape[0]
    rows = 2 * half
    owner = lax.axis_index("ctx")
    core = lax.rem(owner, 2)
    opening = (owner - core) * half
    label = jnp.arange(128, dtype=jnp.int32) % 64
    label = jnp.stack([label, label + 1])
    edges = jnp.sum((segments[None, None, :] < label[:, :, None]).astype(jnp.int32), axis=2)
    edges = edges - (opening - 2 * rows)
    plan = jnp.stack([core, lax.axis_index("head")])

    mate_queries = swapped(queries)
    older = jnp.concatenate([later(latent, 2), later(latent, 1)])
    mine = everywhere(latent)
    mate = [swapped(jnp.concatenate(mine))]
    older, plan, edges = lax.optimization_barrier((older, plan, edges))
    older_mine = everywhere(older)
    state = attention(plan, edges, queries, mate_queries, w_uk, w_uv, mine, mate, None)
    older_mate = [swapped(older_mine[0])]
    state, arrived = lax.optimization_barrier((state, older_mine[1:]))
    older_mine = [older_mine[0], *arrived]
    older_mate += [swapped(x) for x in arrived]
    own, send = attention(
        plan, edges, queries, mate_queries, w_uk, w_uv, older_mine, older_mate, state
    )
    columns = send.shape[1]
    return lax.dynamic_update_slice(own, swapped(send), (0, (1 - core) * columns))


def solution(mesh):
    placed = (
        P(("dp", "ctx"), "head"),
        P(("dp", "ctx", "head"), None),
        P("dp"),
        P("head", None, None),
        P("head", None, None),
    )
    return jax.shard_map(
        on_device, mesh=mesh, in_specs=placed, out_specs=P(("dp", "ctx"), "head"), check_vma=False
    )
```

```python
import functools
import math

import jax
import jax.numpy as jnp
from jax import lax
from jax.experimental import pallas as pl
from jax.experimental.pallas import tpu as pltpu
from jax.sharding import PartitionSpec as P

NOPE = 128
ROPE = 64
LAT = 512
VDIM = 128
DOCS = 12
SCALE = math.log2(math.e) / math.sqrt(NOPE + ROPE)
FAR = -1e30
TILE = 256
WIDE = 512
NT = (((1,), (1,)), ((), ()))
f32, bf16 = jnp.float32, jnp.bfloat16


def attention_kernel(diagonal, blocks, pairs, *refs):
    plan_ref, segment_ref, own_q, mate_q, uk_ref, uv_ref = refs[:6]
    mine = refs[6:10]
    if diagonal:
        piece = mine[0].shape[0]
        mate = [refs[10].at[k * piece : (k + 1) * piece] for k in range(4)]
        refs = refs[11:]
    else:
        mate, refs = refs[10:14], refs[14:]
    if diagonal:
        out_mean, out_weight = refs[:2]
        refs = refs[2:]
    else:
        in_mean, in_weight, out_ref, send_ref = refs[:4]
        weight_refs, refs = refs[4:6], refs[6:]
        sum_ref, total_ref, bound_ref = refs[10:]
    edges_ref, lat_ref, tail_ref, qcat_ref = refs[:4]
    score_refs, value_refs, top_refs = refs[4:6], refs[6:8], refs[8:10]
    step = pl.program_id(0)
    half = own_q.shape[0]
    rows = 2 * half
    past = 2 * rows
    base = past if diagonal else 0
    core, column = plan_ref[0], plan_ref[1]

    @pl.when(step == 0)
    def _():
        piece = mine[0].shape[0] // blocks
        for kind, group in ((core, mine), (1 - core, mate)):
            for ring, ref in zip((0, 3, 1, 2), group):
                slot = lax.rem(column + ring, 4)
                for block in range(blocks):
                    first = pl.multiple_of(block * rows + kind * half + slot * piece, 16)
                    lat_ref[pl.ds(first, piece), :] = ref[block * piece : (block + 1) * piece]
        segment = segment_ref[...]
        below = [jnp.sum(jnp.where(segment < doc, 1.0, 0.0)) for doc in range(1, DOCS)]
        below = [0.0, *below, float(segment.size)]
        label = lax.broadcasted_iota(jnp.int32, (1, 128), 1) & 63
        lows = highs = jnp.full((1, 128), below[DOCS], f32)
        for doc in range(DOCS):
            lows = jnp.where(label == doc, below[doc], lows)
            highs = jnp.where(label == doc, below[doc + 1], highs)
        opening = (plan_ref[2] - past).astype(f32)
        lows, highs = lows - opening, highs - opening
        edges_ref[:1] = lows.astype(jnp.int32)
        edges_ref[1:] = highs.astype(jnp.int32)
        keys = lat_ref.shape[0]
        rope = lat_ref[:, LAT:].astype(f32) * SCALE
        at = lax.broadcasted_iota(jnp.int32, (keys, ROPE), 0) + base
        inside = (at >= edges_ref[:1, :ROPE]) & (at < edges_ref[1:, :ROPE])
        far = jnp.where(inside, 0.0, FAR).astype(f32)
        tail_ref[0] = jnp.concatenate([rope, far], axis=1).astype(bf16)
        tail_ref[1] = jnp.concatenate([far, rope], axis=1).astype(bf16)
        if not diagonal:
            begin = jnp.max(jnp.where(lows <= past, lows, -1e9)).astype(jnp.int32)
            finish = jnp.min(jnp.where(highs > past, highs, 1e9)).astype(jnp.int32)
            bound_ref[0] = lax.div(past - begin + WIDE - 1, WIDE)
            bound_ref[1] = finish - past

    def scores(head, first, size, keys, low, high):
        joined = jnp.concatenate(
            [keys[:, head * 128 : head * 128 + 128], tail_ref[head, pl.ds(first, size), :]], axis=1
        )
        return lax.dot_general(qcat_ref[head, low:high], joined, NT, preferred_element_type=f32)

    def keep(now, head, first, low, high, score, fresh):
        parts = [score[:, k : k + 128] for k in range(0, score.shape[1], 128)]
        best = parts[0]
        for part in parts[1:]:
            best = jnp.maximum(best, part)
        if not fresh:
            best = jnp.maximum(top_refs[now][head, low:high], best)
        top_refs[now][head, low:high] = best
        for k, part in enumerate(parts):
            score_refs[now][head, first // 128 + k, low:high] = part

    def project(now, first, size, wide_uk, wide_uv):
        piece = lat_ref[pl.ds(first, size), :LAT]
        keys = lax.dot_general(piece, wide_uk, NT, preferred_element_type=f32)
        values = jnp.dot(piece, wide_uv, preferred_element_type=f32)
        value_refs[now][pl.ds(first, size), :] = values.astype(bf16)
        return (keys * SCALE).astype(bf16)

    def weigh(before, head, first, size, low, high):
        top = top_refs[before][head, low:high]
        weights = [
            jnp.exp2(score_refs[before][head, first // 128 + k, low:high] - top)
            for k in range(size // 128)
        ]
        values = value_refs[before][pl.ds(first, size), head * 128 : head * 128 + 128]
        both = jnp.dot(
            jnp.concatenate([x.astype(bf16) for x in weights], axis=1),
            jnp.concatenate([values, jnp.ones((size, 128), bf16)], axis=1),
            preferred_element_type=f32,
        )
        return both[:, :128], both[:, 128:]

    def work(now, projecting, weighing):
        before = 1 - now
        if projecting:
            lane = lax.broadcasted_iota(jnp.int32, (rows, 128), 1)
            small = lane < 64
            at = lax.broadcasted_iota(jnp.int32, (rows, 128), 0) + past
            inside = (at >= edges_ref[:1]) & (at < edges_ref[1:])
            doc = jnp.where(inside, 1.0, 0.0).astype(bf16)
            own, other = own_q[...], mate_q[...]
            lead = core == 0
            whole = jnp.concatenate(
                [jnp.where(lead, own, other), jnp.where(lead, other, own)], axis=0
            )
            left, mid, right = whole[:, :128], whole[:, 128:256], whole[:, 256:]
            qcat_ref[0] = jnp.concatenate([left, jnp.where(small, mid, doc)], axis=1)
            qcat_ref[1] = jnp.concatenate(
                [jnp.where(small, right, mid), jnp.where(small, doc, right)], axis=1
            )
            wide_uk = jnp.concatenate([uk_ref[0], uk_ref[1, 64:], uk_ref[1, :64]], axis=0)
            wide_uv = jnp.concatenate([uv_ref[0], uv_ref[1]], axis=1)
        if diagonal:
            for low in range(0, rows, TILE):
                for head in range(2 if weighing else 0):
                        high = low + TILE
                        sums, total = weigh(before, head, 0, high, low, high)
                        out_mean[head, low:high] = sums * (1.0 / total)
                        out_weight[head, low:high] = top_refs[before][head, low:high] + jnp.log2(total)
            if projecting:
                keys = project(now, 0, rows, wide_uk, wide_uv)
            for low in range(0, rows, TILE):
                for head in range(2 if projecting else 0):
                        score = scores(head, low, TILE, keys[low : low + TILE], low, rows)
                        row = lax.broadcasted_iota(jnp.int32, (TILE, TILE), 0)
                        col = lax.broadcasted_iota(jnp.int32, (TILE, TILE), 1)
                        edge = jnp.where(col <= row, score[:TILE], FAR)
                        if low + TILE < rows:
                            edge = jnp.concatenate([edge, score[TILE:]], axis=0)
                        keep(now, head, low, low, rows, edge, low == 0)
        else:
            for head in range(2):
                if projecting:
                    top_refs[now][head] = in_weight[head]
                    weight_refs[now][head] = in_weight[head]
                if weighing:
                    scale = jnp.exp2(weight_refs[before][head] - top_refs[before][head])
                    sum_ref[head] = in_mean[head] * scale
                    total_ref[head] = scale

            def earlier(high):
                def body(turn, carry):
                    first = pl.multiple_of(past - (turn + 1) * WIDE, WIDE)
                    for head in range(2 if weighing else 0):
                        sums, total = weigh(before, head, first, WIDE, 0, high)
                        sum_ref[head, :high] = sum_ref[head, :high] + sums
                        total_ref[head, :high] = total_ref[head, :high] + total
                    if projecting:
                        keys = project(now, first, WIDE, wide_uk, wide_uv)
                    for head in range(2 if projecting else 0):
                        score = scores(head, first, WIDE, keys, 0, high)
                        keep(now, head, first, 0, high, score, False)
                    return carry

                lax.fori_loop(0, bound_ref[0], body, 0)

            reach = bound_ref[1]
            for high in range(TILE, rows + 1, TILE):
                fits = reach > high - TILE
                if high < rows:
                    fits = fits & (reach <= high)
                pl.when(fits)(functools.partial(earlier, high))

        if projecting:
            for head in range(2):
                best = jnp.max(top_refs[now][head], axis=1, keepdims=True)
                top_refs[now][head] = jnp.broadcast_to(best, (rows, 128))
        if weighing and not diagonal:
            for head in range(2):
                ready = (sum_ref[head] * (1.0 / total_ref[head])).astype(bf16)
                at = slice(head * 128, head * 128 + 128)
                out_ref[:, at] = jnp.where(core == 0, ready[:half], ready[half:])
                send_ref[:, at] = jnp.where(core == 0, ready[half:], ready[:half])

    pl.when(step == 0)(functools.partial(work, 0, True, False))
    for parity in range(2):
        inner = (step > 0) & (step < pairs) & (lax.rem(step, 2) == parity)
        pl.when(inner)(functools.partial(work, parity, True, True))
    pl.when(step == pairs)(functools.partial(work, pairs % 2, False, True))


def attention(plan, segments, queries, mate_queries, w_uk, w_uv, mine, mate, state):
    half = queries.shape[0]
    rows = 2 * half
    heads = w_uk.shape[0]
    pairs = heads // 4
    last = pairs - 1
    diagonal = state is None
    blocks = 1 if diagonal else 2
    span = blocks * rows
    whole = lambda x: pl.BlockSpec(x.shape, lambda i, n: (0,) * x.ndim)
    pair = lambda i, n: n[0] * pairs + jnp.minimum(i, last)
    done = lambda i: jnp.maximum(i - 1, 0)
    query = pl.BlockSpec((half, 2 * (NOPE + ROPE)), lambda i, n: (0, pair(i, n)))
    part = pl.BlockSpec((2, rows, 128), lambda i, n: (done(i), 0, 0))
    coming = pl.BlockSpec((2, rows, 128), lambda i, n: (jnp.minimum(i, last), 0, 0))
    scratch = [
        pltpu.VMEM((2, 128), jnp.int32),
        pltpu.VMEM((span, LAT + ROPE), bf16),
        pltpu.VMEM((2, span, 128), bf16),
        pltpu.VMEM((2, rows, 256), bf16),
        *[pltpu.VMEM((2, span // 128, rows, 128), f32)] * 2,
        *[pltpu.VMEM((span, 256), bf16)] * 2,
        *[pltpu.VMEM((2, rows, 128), f32)] * 2,
    ]
    if diagonal:
        extra, more = [], []
        out_specs = [part] * 2
        out_shape = [jax.ShapeDtypeStruct((heads // 2, rows, 128), f32)] * 2
    else:
        extra, more = [part, coming], state
        scratch = [pltpu.VMEM((2, rows, 128), f32)] * 2 + scratch
        scratch += [pltpu.VMEM((2, rows, 128), f32)] * 2 + [pltpu.SMEM((2,), jnp.int32)]
        out_specs = [
            pl.BlockSpec((half, 2 * VDIM), lambda i, n: (0, n[0] * pairs + done(i))),
            pl.BlockSpec((half, 2 * VDIM), lambda i, n: (0, done(i))),
        ]
        out_shape = [
            jax.ShapeDtypeStruct((half, heads * VDIM), bf16),
            jax.ShapeDtypeStruct((half, heads * VDIM // 2), bf16),
        ]
    return pl.pallas_call(
        functools.partial(attention_kernel, diagonal, blocks, pairs),
        grid_spec=pltpu.PrefetchScalarGridSpec(
            num_scalar_prefetch=1,
            grid=(pairs + 1,),
            in_specs=[
                whole(segments),
                query,
                query,
                pl.BlockSpec((2, NOPE, LAT), lambda i, n: (pair(i, n), 0, 0)),
                pl.BlockSpec((2, LAT, VDIM), lambda i, n: (pair(i, n), 0, 0)),
                *[whole(x) for x in mine],
                *[whole(x) for x in mate],
                *extra,
            ],
            out_specs=out_specs,
            scratch_shapes=scratch,
        ),
        out_shape=out_shape,
        compiler_params=pltpu.CompilerParams(vmem_limit_bytes=60 << 20),
        cost_estimate=pl.CostEstimate(
            flops=16 << 30, bytes_accessed=16 << 20, transcendentals=rows * span * heads // 2
        ),
        name="diagonal_attention" if diagonal else "earlier_attention",
    )(plan, segments, queries, mate_queries, w_uk, w_uv, *mine, *mate, *more)


def swapped(x):
    size = lax.axis_size("ctx")
    return lax.ppermute(x, "ctx", [(i, i ^ 1) for i in range(size)])


def later(x, chips):
    size = lax.axis_size("ctx")
    return lax.ppermute(x, "ctx", [(i, i + 2 * chips) for i in range(size - 2 * chips)])


def around(x, by):
    size = lax.axis_size("head")
    return lax.ppermute(x, "head", [(i, (i + by) % size) for i in range(size)])


def everywhere(x):
    return [x, around(x, 1), around(x, -1), around(x, 2)]


def on_device(queries, latent, segments, w_uk, w_uv):
    half = queries.shape[0]
    rows = 2 * half
    owner = lax.axis_index("ctx")
    core = lax.rem(owner, 2)
    opening = (owner - core) * half
    plan = jnp.stack([core, lax.axis_index("head"), opening])
    segments = segments.reshape(-1, 128)

    mate_queries = swapped(queries)
    mine = everywhere(latent)
    farther, nearer = later(latent, 2), later(latent, 1)
    mine, farther, nearer, mate_queries = lax.optimization_barrier(
        (mine, farther, nearer, mate_queries)
    )
    older = jnp.concatenate([farther, nearer])
    mate = [swapped(jnp.concatenate(mine))]
    older_mine = everywhere(older)
    state = attention(plan, segments, queries, mate_queries, w_uk, w_uv, mine, mate, None)
    older_mate = [swapped(older_mine[0])]
    state, arrived = lax.optimization_barrier((state, older_mine[1:]))
    older_mine = [older_mine[0], *arrived]
    older_mate += [swapped(x) for x in arrived]
    own, send = attention(
        plan, segments, queries, mate_queries, w_uk, w_uv, older_mine, older_mate, state
    )
    columns = send.shape[1]
    return lax.dynamic_update_slice(own, swapped(send), (0, (1 - core) * columns))


def solution(mesh):
    placed = (
        P(("dp", "ctx"), "head"),
        P(("dp", "ctx", "head"), None),
        P("dp"),
        P("head", None, None),
        P("head", None, None),
    )
    return jax.shard_map(
        on_device, mesh=mesh, in_specs=placed, out_specs=P(("dp", "ctx"), "head"), check_vma=False
    )
```

```python
import functools
import math

import jax
import jax.numpy as jnp
from jax import lax
from jax.experimental import pallas as pl
from jax.experimental.pallas import tpu as pltpu
from jax.sharding import PartitionSpec as P

NOPE = 128
ROPE = 64
LAT = 512
VDIM = 128
DOCS = 12
SCALE = math.log2(math.e) / math.sqrt(NOPE + ROPE)
FAR = -1e30
TILE = 256
WIDE = 512
NT = (((1,), (1,)), ((), ()))
f32, bf16 = jnp.float32, jnp.bfloat16


def attention_kernel(diagonal, blocks, pairs, *refs):
    plan_ref, segment_ref, own_q, mate_q, uk_ref, uv_ref = refs[:6]
    mine = refs[6:10]
    if diagonal:
        piece = mine[0].shape[0]
        mate = [refs[10].at[k * piece : (k + 1) * piece] for k in range(4)]
        refs = refs[11:]
    else:
        mate, refs = refs[10:14], refs[14:]
    if diagonal:
        out_mean, out_weight = refs[:2]
        refs = refs[2:]
    else:
        in_mean, in_weight, out_ref, send_ref = refs[:4]
        weight_refs, refs = refs[4:6], refs[6:]
        sum_ref, total_ref, bound_ref = refs[10:]
    edges_ref, lat_ref, tail_ref, qcat_ref = refs[:4]
    score_refs, value_refs, top_refs = refs[4:6], refs[6:8], refs[8:10]
    step = pl.program_id(0)
    half = own_q.shape[0]
    rows = 2 * half
    past = 2 * rows
    base = past if diagonal else 0
    core, column = plan_ref[0], plan_ref[1]

    @pl.when(step == 0)
    def _():
        piece = mine[0].shape[0] // blocks
        for kind, group in ((core, mine), (1 - core, mate)):
            for ring, ref in zip((0, 3, 1, 2), group):
                slot = lax.rem(column + ring, 4)
                for block in range(blocks):
                    first = pl.multiple_of(block * rows + kind * half + slot * piece, 16)
                    lat_ref[pl.ds(first, piece), :] = ref[block * piece : (block + 1) * piece]
        segment = segment_ref[...]
        below = [jnp.sum(jnp.where(segment < doc, 1.0, 0.0)) for doc in range(1, DOCS)]
        below = [0.0, *below, float(segment.size)]
        label = lax.broadcasted_iota(jnp.int32, (1, 128), 1) & 63
        lows = highs = jnp.full((1, 128), below[DOCS], f32)
        for doc in range(DOCS):
            lows = jnp.where(label == doc, below[doc], lows)
            highs = jnp.where(label == doc, below[doc + 1], highs)
        opening = (plan_ref[2] - past).astype(f32)
        lows, highs = lows - opening, highs - opening
        edges_ref[:1] = lows.astype(jnp.int32)
        edges_ref[1:] = highs.astype(jnp.int32)
        keys = lat_ref.shape[0]
        rope = lat_ref[:, LAT:].astype(f32) * SCALE
        at = lax.broadcasted_iota(jnp.int32, (keys, ROPE), 0) + base
        inside = (at >= edges_ref[:1, :ROPE]) & (at < edges_ref[1:, :ROPE])
        far = jnp.where(inside, 0.0, FAR).astype(f32)
        tail_ref[0] = jnp.concatenate([rope, far], axis=1).astype(bf16)
        tail_ref[1] = jnp.concatenate([far, rope], axis=1).astype(bf16)
        if not diagonal:
            begin = jnp.max(jnp.where(lows <= past, lows, -1e9)).astype(jnp.int32)
            finish = jnp.min(jnp.where(highs > past, highs, 1e9)).astype(jnp.int32)
            bound_ref[0] = lax.div(past - begin + WIDE - 1, WIDE)
            bound_ref[1] = finish - past

    def scores(head, first, size, keys, low, high):
        joined = jnp.concatenate(
            [keys[:, head * 128 : head * 128 + 128], tail_ref[head, pl.ds(first, size), :]], axis=1
        )
        return lax.dot_general(qcat_ref[head, low:high], joined, NT, preferred_element_type=f32)

    def keep(now, head, first, low, high, score, fresh):
        parts = [score[:, k : k + 128] for k in range(0, score.shape[1], 128)]
        best = parts[0]
        for part in parts[1:]:
            best = jnp.maximum(best, part)
        if not fresh:
            best = jnp.maximum(top_refs[now][head, low:high], best)
        top_refs[now][head, low:high] = best
        for k, part in enumerate(parts):
            score_refs[now][head, first // 128 + k, low:high] = part

    def project(now, first, size, wide_uk, wide_uv):
        piece = lat_ref[pl.ds(first, size), :LAT]
        keys = lax.dot_general(piece, wide_uk, NT, preferred_element_type=f32)
        values = jnp.dot(piece, wide_uv, preferred_element_type=f32)
        value_refs[now][pl.ds(first, size), :] = values.astype(bf16)
        return (keys * SCALE).astype(bf16)

    def weigh(before, head, first, size, low, high):
        top = top_refs[before][head, low:high]
        weights = [
            jnp.exp2(score_refs[before][head, first // 128 + k, low:high] - top)
            for k in range(size // 128)
        ]
        values = value_refs[before][pl.ds(first, size), head * 128 : head * 128 + 128]
        both = jnp.dot(
            jnp.concatenate([x.astype(bf16) for x in weights], axis=1),
            jnp.concatenate([values, jnp.ones((size, 128), bf16)], axis=1),
            preferred_element_type=f32,
        )
        return both[:, :128], both[:, 128:]

    def work(now, projecting, weighing):
        before = 1 - now
        if projecting:
            lane = lax.broadcasted_iota(jnp.int32, (rows, 128), 1)
            small = lane < 64
            at = lax.broadcasted_iota(jnp.int32, (rows, 128), 0) + past
            inside = (at >= edges_ref[:1]) & (at < edges_ref[1:])
            doc = jnp.where(inside, 1.0, 0.0).astype(bf16)
            own, other = own_q[...], mate_q[...]
            lead = core == 0
            whole = jnp.concatenate(
                [jnp.where(lead, own, other), jnp.where(lead, other, own)], axis=0
            )
            left, mid, right = whole[:, :128], whole[:, 128:256], whole[:, 256:]
            qcat_ref[0] = jnp.concatenate([left, jnp.where(small, mid, doc)], axis=1)
            qcat_ref[1] = jnp.concatenate(
                [jnp.where(small, right, mid), jnp.where(small, doc, right)], axis=1
            )
            wide_uk = jnp.concatenate([uk_ref[0], uk_ref[1, 64:], uk_ref[1, :64]], axis=0)
            wide_uv = jnp.concatenate([uv_ref[0], uv_ref[1]], axis=1)
        if diagonal:
            for low in range(0, rows, TILE):
                for head in range(2 if weighing else 0):
                        high = low + TILE
                        sums, total = weigh(before, head, 0, high, low, high)
                        out_mean[head, low:high] = sums * (1.0 / total)
                        out_weight[head, low:high] = top_refs[before][head, low:high] + jnp.log2(total)
            if projecting:
                keys = project(now, 0, rows, wide_uk, wide_uv)
            for low in range(0, rows, TILE):
                for head in range(2 if projecting else 0):
                        score = scores(head, low, TILE, keys[low : low + TILE], low, rows)
                        row = lax.broadcasted_iota(jnp.int32, (TILE, TILE), 0)
                        col = lax.broadcasted_iota(jnp.int32, (TILE, TILE), 1)
                        edge = jnp.where(col <= row, score[:TILE], FAR)
                        if low + TILE < rows:
                            edge = jnp.concatenate([edge, score[TILE:]], axis=0)
                        keep(now, head, low, low, rows, edge, low == 0)
        else:
            for head in range(2):
                if projecting:
                    top_refs[now][head] = in_weight[head]
                    weight_refs[now][head] = in_weight[head]
                if weighing:
                    scale = jnp.exp2(weight_refs[before][head] - top_refs[before][head])
                    sum_ref[head] = in_mean[head] * scale
                    total_ref[head] = scale

            def earlier(high):
                def body(turn, carry):
                    first = pl.multiple_of(past - (turn + 1) * WIDE, WIDE)
                    for head in range(2 if weighing else 0):
                        sums, total = weigh(before, head, first, WIDE, 0, high)
                        sum_ref[head, :high] = sum_ref[head, :high] + sums
                        total_ref[head, :high] = total_ref[head, :high] + total
                    if projecting:
                        keys = project(now, first, WIDE, wide_uk, wide_uv)
                    for head in range(2 if projecting else 0):
                        score = scores(head, first, WIDE, keys, 0, high)
                        keep(now, head, first, 0, high, score, False)
                    return carry

                lax.fori_loop(0, bound_ref[0], body, 0)

            reach = bound_ref[1]
            for high in range(TILE, rows + 1, TILE):
                fits = reach > high - TILE
                if high < rows:
                    fits = fits & (reach <= high)
                pl.when(fits)(functools.partial(earlier, high))

        if projecting:
            for head in range(2):
                best = jnp.max(top_refs[now][head], axis=1, keepdims=True)
                top_refs[now][head] = jnp.broadcast_to(best, (rows, 128))
        if weighing and not diagonal:
            for head in range(2):
                ready = (sum_ref[head] * (1.0 / total_ref[head])).astype(bf16)
                at = slice(head * 128, head * 128 + 128)
                out_ref[:, at] = jnp.where(core == 0, ready[:half], ready[half:])
                send_ref[:, at] = jnp.where(core == 0, ready[half:], ready[:half])

    pl.when(step == 0)(functools.partial(work, 0, True, False))
    for parity in range(2):
        inner = (step > 0) & (step < pairs) & (lax.rem(step, 2) == parity)
        pl.when(inner)(functools.partial(work, parity, True, True))
    pl.when(step == pairs)(functools.partial(work, pairs % 2, False, True))


def attention(plan, segments, queries, mate_queries, w_uk, w_uv, mine, mate, state):
    half = queries.shape[0]
    rows = 2 * half
    heads = w_uk.shape[0]
    pairs = heads // 4
    last = pairs - 1
    diagonal = state is None
    blocks = 1 if diagonal else 2
    span = blocks * rows
    whole = lambda x: pl.BlockSpec(x.shape, lambda i, n: (0,) * x.ndim)
    pair = lambda i, n: n[0] * pairs + jnp.minimum(i, last)
    done = lambda i: jnp.maximum(i - 1, 0)
    query = pl.BlockSpec((half, 2 * (NOPE + ROPE)), lambda i, n: (0, pair(i, n)))
    part = pl.BlockSpec((2, rows, 128), lambda i, n: (done(i), 0, 0))
    coming = pl.BlockSpec((2, rows, 128), lambda i, n: (jnp.minimum(i, last), 0, 0))
    scratch = [
        pltpu.VMEM((2, 128), jnp.int32),
        pltpu.VMEM((span, LAT + ROPE), bf16),
        pltpu.VMEM((2, span, 128), bf16),
        pltpu.VMEM((2, rows, 256), bf16),
        *[pltpu.VMEM((2, span // 128, rows, 128), f32)] * 2,
        *[pltpu.VMEM((span, 256), bf16)] * 2,
        *[pltpu.VMEM((2, rows, 128), f32)] * 2,
    ]
    if diagonal:
        extra, more = [], []
        out_specs = [part] * 2
        out_shape = [jax.ShapeDtypeStruct((heads // 2, rows, 128), f32)] * 2
    else:
        extra, more = [part, coming], state
        scratch = [pltpu.VMEM((2, rows, 128), f32)] * 2 + scratch
        scratch += [pltpu.VMEM((2, rows, 128), f32)] * 2 + [pltpu.SMEM((2,), jnp.int32)]
        out_specs = [
            pl.BlockSpec((half, 2 * VDIM), lambda i, n: (0, n[0] * pairs + done(i))),
            pl.BlockSpec((half, 2 * VDIM), lambda i, n: (0, done(i))),
        ]
        out_shape = [
            jax.ShapeDtypeStruct((half, heads * VDIM), bf16),
            jax.ShapeDtypeStruct((half, heads * VDIM // 2), bf16),
        ]
    return pl.pallas_call(
        functools.partial(attention_kernel, diagonal, blocks, pairs),
        grid_spec=pltpu.PrefetchScalarGridSpec(
            num_scalar_prefetch=1,
            grid=(pairs + 1,),
            in_specs=[
                whole(segments),
                query,
                query,
                pl.BlockSpec((2, NOPE, LAT), lambda i, n: (pair(i, n), 0, 0)),
                pl.BlockSpec((2, LAT, VDIM), lambda i, n: (pair(i, n), 0, 0)),
                *[whole(x) for x in mine],
                *[whole(x) for x in mate],
                *extra,
            ],
            out_specs=out_specs,
            scratch_shapes=scratch,
        ),
        out_shape=out_shape,
        compiler_params=pltpu.CompilerParams(vmem_limit_bytes=60 << 20),
        cost_estimate=pl.CostEstimate(
            flops=16 << 30, bytes_accessed=16 << 20, transcendentals=rows * span * heads // 2
        ),
        name="diagonal_attention" if diagonal else "earlier_attention",
    )(plan, segments, queries, mate_queries, w_uk, w_uv, *mine, *mate, *more)


def swapped(x):
    size = lax.axis_size("ctx")
    return lax.ppermute(x, "ctx", [(i, i ^ 1) for i in range(size)])


def later(x, chips):
    size = lax.axis_size("ctx")
    return lax.ppermute(x, "ctx", [(i, i + 2 * chips) for i in range(size - 2 * chips)])


def around(x, by):
    size = lax.axis_size("head")
    return lax.ppermute(x, "head", [(i, (i + by) % size) for i in range(size)])


def everywhere(x):
    return [x, around(x, 1), around(x, -1), around(x, 2)]


def on_device(queries, latent, segments, w_uk, w_uv):
    half = queries.shape[0]
    rows = 2 * half
    owner = lax.axis_index("ctx")
    core = lax.rem(owner, 2)
    opening = (owner - core) * half
    plan = jnp.stack([core, lax.axis_index("head"), opening])
    segments = segments.reshape(-1, 128)

    mine = everywhere(latent)
    farther, nearer = later(latent, 2), later(latent, 1)
    mine, farther, nearer, outgoing = lax.optimization_barrier((mine, farther, nearer, queries))
    mate_queries = swapped(outgoing)
    older = jnp.concatenate([farther, nearer])
    mate = [swapped(jnp.concatenate(mine))]
    older, mate_queries = lax.optimization_barrier((older, mate_queries))
    older_mine = everywhere(older)
    state = attention(plan, segments, queries, mate_queries, w_uk, w_uv, mine, mate, None)
    older_mate = [swapped(older_mine[0])]
    state, arrived = lax.optimization_barrier((state, older_mine[1:]))
    older_mine = [older_mine[0], *arrived]
    older_mate += [swapped(x) for x in arrived]
    own, send = attention(
        plan, segments, queries, mate_queries, w_uk, w_uv, older_mine, older_mate, state
    )
    columns = send.shape[1]
    return lax.dynamic_update_slice(own, swapped(send), (0, (1 - core) * columns))


def solution(mesh):
    placed = (
        P(("dp", "ctx"), "head"),
        P(("dp", "ctx", "head"), None),
        P("dp"),
        P("head", None, None),
        P("head", None, None),
    )
    return jax.shard_map(
        on_device, mesh=mesh, in_specs=placed, out_specs=P(("dp", "ctx"), "head"), check_vma=False
    )
```

```python
import functools
import math

import jax
import jax.numpy as jnp
from jax import lax
from jax.experimental import pallas as pl
from jax.experimental.pallas import tpu as pltpu
from jax.sharding import PartitionSpec as P

NOPE = 128
ROPE = 64
LAT = 512
VDIM = 128
DOCS = 12
SCALE = math.log2(math.e) / math.sqrt(NOPE + ROPE)
FAR = -1e30
TILE = 256
WIDE = 512
NT = (((1,), (1,)), ((), ()))
f32, bf16 = jnp.float32, jnp.bfloat16


def attention_kernel(diagonal, blocks, pairs, *refs):
    plan_ref, segment_ref, own_q, mate_q, uk_ref, uv_ref = refs[:6]
    mine = refs[6:10]
    if diagonal:
        piece = mine[0].shape[0]
        mate = [refs[10].at[k * piece : (k + 1) * piece] for k in range(4)]
        refs = refs[11:]
    else:
        mate, refs = refs[10:14], refs[14:]
    if diagonal:
        out_mean, out_weight = refs[:2]
        refs = refs[2:]
    else:
        in_mean, in_weight, out_ref, send_ref = refs[:4]
        weight_refs, refs = refs[4:6], refs[6:]
        sum_ref, total_ref, bound_ref = refs[10:]
    edges_ref, lat_ref, tail_ref, qcat_ref = refs[:4]
    score_refs, value_refs, top_refs = refs[4:6], refs[6:8], refs[8:10]
    step = pl.program_id(0)
    half = own_q.shape[0]
    rows = 2 * half
    past = 2 * rows
    base = past if diagonal else 0
    core, column = plan_ref[0], plan_ref[1]

    @pl.when(step == 0)
    def _():
        piece = mine[0].shape[0] // blocks
        for kind, group in ((core, mine), (1 - core, mate)):
            for ring, ref in zip((0, 3, 1, 2), group):
                slot = lax.rem(column + ring, 4)
                for block in range(blocks):
                    first = pl.multiple_of(block * rows + kind * half + slot * piece, 16)
                    lat_ref[pl.ds(first, piece), :] = ref[block * piece : (block + 1) * piece]
        segment = segment_ref[...]
        below = [jnp.sum(jnp.where(segment < doc, 1.0, 0.0)) for doc in range(1, DOCS)]
        below = [0.0, *below, float(segment.size)]
        label = lax.broadcasted_iota(jnp.int32, (1, 128), 1) & 63
        lows = highs = jnp.full((1, 128), below[DOCS], f32)
        for doc in range(DOCS):
            lows = jnp.where(label == doc, below[doc], lows)
            highs = jnp.where(label == doc, below[doc + 1], highs)
        opening = (plan_ref[2] - past).astype(f32)
        lows, highs = lows - opening, highs - opening
        edges_ref[:1] = lows.astype(jnp.int32)
        edges_ref[1:] = highs.astype(jnp.int32)
        keys = lat_ref.shape[0]
        rope = lat_ref[:, LAT:].astype(f32) * SCALE
        at = lax.broadcasted_iota(jnp.int32, (keys, ROPE), 0) + base
        inside = (at >= edges_ref[:1, :ROPE]) & (at < edges_ref[1:, :ROPE])
        far = jnp.where(inside, 0.0, FAR).astype(f32)
        tail_ref[0] = jnp.concatenate([rope, far], axis=1).astype(bf16)
        tail_ref[1] = jnp.concatenate([far, rope], axis=1).astype(bf16)
        if not diagonal:
            begin = jnp.max(jnp.where(lows <= past, lows, -1e9)).astype(jnp.int32)
            finish = jnp.min(jnp.where(highs > past, highs, 1e9)).astype(jnp.int32)
            bound_ref[0] = lax.div(past - begin + WIDE - 1, WIDE)
            bound_ref[1] = finish - past

    def scores(head, first, size, keys, low, high):
        joined = jnp.concatenate(
            [keys[:, head * 128 : head * 128 + 128], tail_ref[head, pl.ds(first, size), :]], axis=1
        )
        return lax.dot_general(qcat_ref[head, low:high], joined, NT, preferred_element_type=f32)

    def keep(now, head, first, low, high, score, fresh):
        parts = [score[:, k : k + 128] for k in range(0, score.shape[1], 128)]
        best = parts[0]
        for part in parts[1:]:
            best = jnp.maximum(best, part)
        if not fresh:
            best = jnp.maximum(top_refs[now][head, low:high], best)
        top_refs[now][head, low:high] = best
        for k, part in enumerate(parts):
            score_refs[now][head, first // 128 + k, low:high] = part

    def project(now, first, size, wide_uk, wide_uv):
        piece = lat_ref[pl.ds(first, size), :LAT]
        keys = lax.dot_general(piece, wide_uk, NT, preferred_element_type=f32)
        values = jnp.dot(piece, wide_uv, preferred_element_type=f32)
        value_refs[now][pl.ds(first, size), :] = values.astype(bf16)
        return (keys * SCALE).astype(bf16)

    def weigh(before, head, first, size, low, high):
        top = top_refs[before][head, low:high]
        weights = [
            jnp.exp2(score_refs[before][head, first // 128 + k, low:high] - top)
            for k in range(size // 128)
        ]
        values = value_refs[before][pl.ds(first, size), head * 128 : head * 128 + 128]
        both = jnp.dot(
            jnp.concatenate([x.astype(bf16) for x in weights], axis=1),
            jnp.concatenate([values, jnp.ones((size, 128), bf16)], axis=1),
            preferred_element_type=f32,
        )
        return both[:, :128], both[:, 128:]

    def work(now, projecting, weighing):
        before = 1 - now
        if projecting:
            lane = lax.broadcasted_iota(jnp.int32, (rows, 128), 1)
            small = lane < 64
            at = lax.broadcasted_iota(jnp.int32, (rows, 128), 0) + past
            inside = (at >= edges_ref[:1]) & (at < edges_ref[1:])
            doc = jnp.where(inside, 1.0, 0.0).astype(bf16)
            own, other = own_q[...], mate_q[...]
            lead = core == 0
            whole = jnp.concatenate(
                [jnp.where(lead, own, other), jnp.where(lead, other, own)], axis=0
            )
            left, mid, right = whole[:, :128], whole[:, 128:256], whole[:, 256:]
            qcat_ref[0] = jnp.concatenate([left, jnp.where(small, mid, doc)], axis=1)
            qcat_ref[1] = jnp.concatenate(
                [jnp.where(small, right, mid), jnp.where(small, doc, right)], axis=1
            )
            wide_uk = jnp.concatenate([uk_ref[0], uk_ref[1, 64:], uk_ref[1, :64]], axis=0)
            wide_uv = jnp.concatenate([uv_ref[0], uv_ref[1]], axis=1)
        if diagonal:
            for low in range(0, rows, TILE):
                for head in range(2 if weighing else 0):
                        high = low + TILE
                        sums, total = weigh(before, head, 0, high, low, high)
                        out_mean[head, low:high] = sums * (1.0 / total)
                        out_weight[head, low:high] = top_refs[before][head, low:high] + jnp.log2(total)
            if projecting:
                keys = project(now, 0, rows, wide_uk, wide_uv)
            for low in range(0, rows, TILE):
                for head in range(2 if projecting else 0):
                        score = scores(head, low, TILE, keys[low : low + TILE], low, rows)
                        row = lax.broadcasted_iota(jnp.int32, (TILE, TILE), 0)
                        col = lax.broadcasted_iota(jnp.int32, (TILE, TILE), 1)
                        edge = jnp.where(col <= row, score[:TILE], FAR)
                        if low + TILE < rows:
                            edge = jnp.concatenate([edge, score[TILE:]], axis=0)
                        keep(now, head, low, low, rows, edge, low == 0)
        else:
            for head in range(2):
                if projecting:
                    top_refs[now][head] = in_weight[head]
                    weight_refs[now][head] = in_weight[head]
                if weighing:
                    scale = jnp.exp2(weight_refs[before][head] - top_refs[before][head])
                    sum_ref[head] = in_mean[head] * scale
                    total_ref[head] = scale

            def earlier(high):
                def body(turn, carry):
                    first = pl.multiple_of(past - (turn + 1) * WIDE, WIDE)
                    for head in range(2 if weighing else 0):
                        sums, total = weigh(before, head, first, WIDE, 0, high)
                        sum_ref[head, :high] = sum_ref[head, :high] + sums
                        total_ref[head, :high] = total_ref[head, :high] + total
                    if projecting:
                        keys = project(now, first, WIDE, wide_uk, wide_uv)
                    for head in range(2 if projecting else 0):
                        score = scores(head, first, WIDE, keys, 0, high)
                        keep(now, head, first, 0, high, score, False)
                    return carry

                lax.fori_loop(0, bound_ref[0], body, 0)

            reach = bound_ref[1]
            for high in range(TILE, rows + 1, TILE):
                fits = reach > high - TILE
                if high < rows:
                    fits = fits & (reach <= high)
                pl.when(fits)(functools.partial(earlier, high))

        if projecting:
            for head in range(2):
                best = jnp.max(top_refs[now][head], axis=1, keepdims=True)
                top_refs[now][head] = jnp.broadcast_to(best, (rows, 128))
        if weighing and not diagonal:
            for head in range(2):
                ready = (sum_ref[head] * (1.0 / total_ref[head])).astype(bf16)
                at = slice(head * 128, head * 128 + 128)
                out_ref[:, at] = jnp.where(core == 0, ready[:half], ready[half:])
                send_ref[:, at] = jnp.where(core == 0, ready[half:], ready[:half])

    pl.when(step == 0)(functools.partial(work, 0, True, False))
    for parity in range(2):
        inner = (step > 0) & (step < pairs) & (lax.rem(step, 2) == parity)
        pl.when(inner)(functools.partial(work, parity, True, True))
    pl.when(step == pairs)(functools.partial(work, pairs % 2, False, True))


def attention(plan, segments, queries, mate_queries, w_uk, w_uv, mine, mate, state):
    half = queries.shape[0]
    rows = 2 * half
    heads = w_uk.shape[0]
    pairs = heads // 4
    last = pairs - 1
    diagonal = state is None
    blocks = 1 if diagonal else 2
    span = blocks * rows
    whole = lambda x: pl.BlockSpec(x.shape, lambda i, n: (0,) * x.ndim)
    pair = lambda i, n: n[0] * pairs + jnp.minimum(i, last)
    done = lambda i: jnp.maximum(i - 1, 0)
    query = pl.BlockSpec((half, 2 * (NOPE + ROPE)), lambda i, n: (0, pair(i, n)))
    part = pl.BlockSpec((2, rows, 128), lambda i, n: (done(i), 0, 0))
    coming = pl.BlockSpec((2, rows, 128), lambda i, n: (jnp.minimum(i, last), 0, 0))
    scratch = [
        pltpu.VMEM((2, 128), jnp.int32),
        pltpu.VMEM((span, LAT + ROPE), bf16),
        pltpu.VMEM((2, span, 128), bf16),
        pltpu.VMEM((2, rows, 256), bf16),
        *[pltpu.VMEM((2, span // 128, rows, 128), f32)] * 2,
        *[pltpu.VMEM((span, 256), bf16)] * 2,
        *[pltpu.VMEM((2, rows, 128), f32)] * 2,
    ]
    if diagonal:
        extra, more = [], []
        out_specs = [part] * 2
        out_shape = [jax.ShapeDtypeStruct((heads // 2, rows, 128), f32)] * 2
    else:
        extra, more = [part, coming], state
        scratch = [pltpu.VMEM((2, rows, 128), f32)] * 2 + scratch
        scratch += [pltpu.VMEM((2, rows, 128), f32)] * 2 + [pltpu.SMEM((2,), jnp.int32)]
        out_specs = [
            pl.BlockSpec((half, 2 * VDIM), lambda i, n: (0, n[0] * pairs + done(i))),
            pl.BlockSpec((half, 2 * VDIM), lambda i, n: (0, done(i))),
        ]
        out_shape = [
            jax.ShapeDtypeStruct((half, heads * VDIM), bf16),
            jax.ShapeDtypeStruct((half, heads * VDIM // 2), bf16),
        ]
    return pl.pallas_call(
        functools.partial(attention_kernel, diagonal, blocks, pairs),
        grid_spec=pltpu.PrefetchScalarGridSpec(
            num_scalar_prefetch=1,
            grid=(pairs + 1,),
            in_specs=[
                whole(segments),
                query,
                query,
                pl.BlockSpec((2, NOPE, LAT), lambda i, n: (pair(i, n), 0, 0)),
                pl.BlockSpec((2, LAT, VDIM), lambda i, n: (pair(i, n), 0, 0)),
                *[whole(x) for x in mine],
                *[whole(x) for x in mate],
                *extra,
            ],
            out_specs=out_specs,
            scratch_shapes=scratch,
        ),
        out_shape=out_shape,
        compiler_params=pltpu.CompilerParams(vmem_limit_bytes=60 << 20),
        cost_estimate=pl.CostEstimate(
            flops=16 << 30, bytes_accessed=16 << 20, transcendentals=rows * span * heads // 2
        ),
        name="diagonal_attention" if diagonal else "earlier_attention",
    )(plan, segments, queries, mate_queries, w_uk, w_uv, *mine, *mate, *more)


def swapped(x):
    size = lax.axis_size("ctx")
    return lax.ppermute(x, "ctx", [(i, i ^ 1) for i in range(size)])


def later(x, chips):
    size = lax.axis_size("ctx")
    return lax.ppermute(x, "ctx", [(i, i + 2 * chips) for i in range(size - 2 * chips)])


def around(x, by):
    size = lax.axis_size("head")
    return lax.ppermute(x, "head", [(i, (i + by) % size) for i in range(size)])


def everywhere(x):
    return [x, around(x, 1), around(x, -1), around(x, 2)]


def on_device(queries, latent, segments, w_uk, w_uv):
    half = queries.shape[0]
    rows = 2 * half
    owner = lax.axis_index("ctx")
    core = lax.rem(owner, 2)
    opening = (owner - core) * half
    plan = jnp.stack([core, lax.axis_index("head"), opening])
    segments = segments.reshape(-1, 128)

    mate_queries = swapped(queries)
    farther = later(latent, 2)
    mine = everywhere(latent)
    outgoing, mate_queries = lax.optimization_barrier((latent, mate_queries))
    nearer = later(outgoing, 1)
    mine, farther, nearer, mate_queries = lax.optimization_barrier(
        (mine, farther, nearer, mate_queries)
    )
    older = jnp.concatenate([farther, nearer])
    mate = [swapped(jnp.concatenate(mine))]
    older_mine = everywhere(older)
    state = attention(plan, segments, queries, mate_queries, w_uk, w_uv, mine, mate, None)
    older_mate = [swapped(older_mine[0])]
    state, arrived = lax.optimization_barrier((state, older_mine[1:]))
    older_mine = [older_mine[0], *arrived]
    older_mate += [swapped(x) for x in arrived]
    own, send = attention(
        plan, segments, queries, mate_queries, w_uk, w_uv, older_mine, older_mate, state
    )
    columns = send.shape[1]
    return lax.dynamic_update_slice(own, swapped(send), (0, (1 - core) * columns))


def solution(mesh):
    placed = (
        P(("dp", "ctx"), "head"),
        P(("dp", "ctx", "head"), None),
        P("dp"),
        P("head", None, None),
        P("head", None, None),
    )
    return jax.shard_map(
        on_device, mesh=mesh, in_specs=placed, out_specs=P(("dp", "ctx"), "head"), check_vma=False
    )
```

```python
import functools
import math

import jax
import jax.numpy as jnp
from jax import lax
from jax.experimental import pallas as pl
from jax.experimental.pallas import tpu as pltpu
from jax.sharding import PartitionSpec as P

NOPE = 128
ROPE = 64
LAT = 512
VDIM = 128
DOCS = 12
SCALE = math.log2(math.e) / math.sqrt(NOPE + ROPE)
FAR = -1e30
TILE = 256
WIDE = 512
NT = (((1,), (1,)), ((), ()))
f32, bf16 = jnp.float32, jnp.bfloat16


def attention_kernel(diagonal, blocks, pairs, *refs):
    plan_ref, segment_ref, own_q, mate_q, uk_ref, uv_ref = refs[:6]
    mine = refs[6:10]
    if diagonal:
        piece = mine[0].shape[0]
        mate = [refs[10].at[k * piece : (k + 1) * piece] for k in range(4)]
        refs = refs[11:]
    else:
        mate, refs = refs[10:14], refs[14:]
    if diagonal:
        out_mean, out_weight = refs[:2]
        refs = refs[2:]
    else:
        in_mean, in_weight, out_ref, send_ref = refs[:4]
        weight_refs, refs = refs[4:6], refs[6:]
        sum_ref, total_ref, bound_ref = refs[10:]
    edges_ref, lat_ref, tail_ref, qcat_ref = refs[:4]
    score_refs, value_refs, top_refs = refs[4:6], refs[6:8], refs[8:10]
    step = pl.program_id(0)
    half = own_q.shape[0]
    rows = 2 * half
    past = 2 * rows
    base = past if diagonal else 0
    core, column = plan_ref[0], plan_ref[1]

    @pl.when(step == 0)
    def _():
        piece = mine[0].shape[0] // blocks
        for kind, group in ((core, mine), (1 - core, mate)):
            for ring, ref in zip((0, 3, 1, 2), group):
                slot = lax.rem(column + ring, 4)
                for block in range(blocks):
                    first = pl.multiple_of(block * rows + kind * half + slot * piece, 16)
                    lat_ref[pl.ds(first, piece), :] = ref[block * piece : (block + 1) * piece]
        segment = segment_ref[...]
        below = [jnp.sum(jnp.where(segment < doc, 1.0, 0.0)) for doc in range(1, DOCS)]
        below = [0.0, *below, float(segment.size)]
        label = lax.broadcasted_iota(jnp.int32, (1, 128), 1) & 63
        lows = highs = jnp.full((1, 128), below[DOCS], f32)
        for doc in range(DOCS):
            lows = jnp.where(label == doc, below[doc], lows)
            highs = jnp.where(label == doc, below[doc + 1], highs)
        opening = (plan_ref[2] - past).astype(f32)
        lows, highs = lows - opening, highs - opening
        edges_ref[:1] = lows.astype(jnp.int32)
        edges_ref[1:] = highs.astype(jnp.int32)
        keys = lat_ref.shape[0]
        rope = lat_ref[:, LAT:].astype(f32) * SCALE
        at = lax.broadcasted_iota(jnp.int32, (keys, ROPE), 0) + base
        inside = (at >= edges_ref[:1, :ROPE]) & (at < edges_ref[1:, :ROPE])
        far = jnp.where(inside, 0.0, FAR).astype(f32)
        tail_ref[0] = jnp.concatenate([rope, far], axis=1).astype(bf16)
        tail_ref[1] = jnp.concatenate([far, rope], axis=1).astype(bf16)
        if not diagonal:
            begin = jnp.max(jnp.where(lows <= past, lows, -1e9)).astype(jnp.int32)
            finish = jnp.min(jnp.where(highs > past, highs, 1e9)).astype(jnp.int32)
            bound_ref[0] = lax.div(past - begin + TILE - 1, TILE)
            bound_ref[1] = finish - past

    def scores(head, first, size, keys, low, high):
        joined = jnp.concatenate(
            [keys[:, head * 128 : head * 128 + 128], tail_ref[head, pl.ds(first, size), :]], axis=1
        )
        return lax.dot_general(qcat_ref[head, low:high], joined, NT, preferred_element_type=f32)

    def keep(now, head, first, low, high, score, fresh):
        parts = [score[:, k : k + 128] for k in range(0, score.shape[1], 128)]
        best = parts[0]
        for part in parts[1:]:
            best = jnp.maximum(best, part)
        if not fresh:
            best = jnp.maximum(top_refs[now][head, low:high], best)
        top_refs[now][head, low:high] = best
        for k, part in enumerate(parts):
            score_refs[now][head, first // 128 + k, low:high] = part

    def project(now, first, size, wide_uk, wide_uv):
        piece = lat_ref[pl.ds(first, size), :LAT]
        keys = lax.dot_general(piece, wide_uk, NT, preferred_element_type=f32)
        values = jnp.dot(piece, wide_uv, preferred_element_type=f32)
        value_refs[now][pl.ds(first, size), :] = values.astype(bf16)
        return (keys * SCALE).astype(bf16)

    def weigh(before, head, first, size, low, high):
        top = top_refs[before][head, low:high]
        weights = [
            jnp.exp2(score_refs[before][head, first // 128 + k, low:high] - top)
            for k in range(size // 128)
        ]
        values = value_refs[before][pl.ds(first, size), head * 128 : head * 128 + 128]
        both = jnp.dot(
            jnp.concatenate([x.astype(bf16) for x in weights], axis=1),
            jnp.concatenate([values, jnp.ones((size, 128), bf16)], axis=1),
            preferred_element_type=f32,
        )
        return both[:, :128], both[:, 128:]

    def work(now, projecting, weighing):
        before = 1 - now
        if projecting:
            lane = lax.broadcasted_iota(jnp.int32, (rows, 128), 1)
            small = lane < 64
            at = lax.broadcasted_iota(jnp.int32, (rows, 128), 0) + past
            inside = (at >= edges_ref[:1]) & (at < edges_ref[1:])
            doc = jnp.where(inside, 1.0, 0.0).astype(bf16)
            own, other = own_q[...], mate_q[...]
            lead = core == 0
            whole = jnp.concatenate(
                [jnp.where(lead, own, other), jnp.where(lead, other, own)], axis=0
            )
            left, mid, right = whole[:, :128], whole[:, 128:256], whole[:, 256:]
            qcat_ref[0] = jnp.concatenate([left, jnp.where(small, mid, doc)], axis=1)
            qcat_ref[1] = jnp.concatenate(
                [jnp.where(small, right, mid), jnp.where(small, doc, right)], axis=1
            )
            wide_uk = jnp.concatenate([uk_ref[0], uk_ref[1, 64:], uk_ref[1, :64]], axis=0)
            wide_uv = jnp.concatenate([uv_ref[0], uv_ref[1]], axis=1)
        if diagonal:
            for low in range(0, rows, TILE):
                for head in range(2 if weighing else 0):
                        high = low + TILE
                        sums, total = weigh(before, head, 0, high, low, high)
                        out_mean[head, low:high] = sums * (1.0 / total)
                        out_weight[head, low:high] = top_refs[before][head, low:high] + jnp.log2(total)
            if projecting:
                keys = project(now, 0, rows, wide_uk, wide_uv)
            for low in range(0, rows, TILE):
                for head in range(2 if projecting else 0):
                        score = scores(head, low, TILE, keys[low : low + TILE], low, rows)
                        row = lax.broadcasted_iota(jnp.int32, (TILE, TILE), 0)
                        col = lax.broadcasted_iota(jnp.int32, (TILE, TILE), 1)
                        edge = jnp.where(col <= row, score[:TILE], FAR)
                        if low + TILE < rows:
                            edge = jnp.concatenate([edge, score[TILE:]], axis=0)
                        keep(now, head, low, low, rows, edge, low == 0)
        else:
            for head in range(2):
                if projecting:
                    top_refs[now][head] = in_weight[head]
                    weight_refs[now][head] = in_weight[head]
                if weighing:
                    scale = jnp.exp2(weight_refs[before][head] - top_refs[before][head])
                    sum_ref[head] = in_mean[head] * scale
                    total_ref[head] = scale

            def earlier(high):
                def tile(first, size):
                    for head in range(2 if weighing else 0):
                        sums, total = weigh(before, head, first, size, 0, high)
                        sum_ref[head, :high] = sum_ref[head, :high] + sums
                        total_ref[head, :high] = total_ref[head, :high] + total
                    if projecting:
                        keys = project(now, first, size, wide_uk, wide_uv)
                    for head in range(2 if projecting else 0):
                        score = scores(head, first, size, keys, 0, high)
                        keep(now, head, first, 0, high, score, False)

                def wide(turn, carry):
                    tile(pl.multiple_of(past - (turn + 1) * WIDE, WIDE), WIDE)
                    return carry

                def rest(turn, carry):
                    tile(pl.multiple_of(past - bound_ref[0] * TILE, TILE), TILE)
                    return carry

                lax.fori_loop(0, lax.div(bound_ref[0], WIDE // TILE), wide, 0)
                lax.fori_loop(0, lax.rem(bound_ref[0], WIDE // TILE), rest, 0)

            reach = bound_ref[1]
            for high in range(TILE, rows + 1, TILE):
                fits = reach > high - TILE
                if high < rows:
                    fits = fits & (reach <= high)
                pl.when(fits)(functools.partial(earlier, high))

        if projecting:
            for head in range(2):
                best = jnp.max(top_refs[now][head], axis=1, keepdims=True)
                top_refs[now][head] = jnp.broadcast_to(best, (rows, 128))
        if weighing and not diagonal:
            for head in range(2):
                ready = (sum_ref[head] * (1.0 / total_ref[head])).astype(bf16)
                at = slice(head * 128, head * 128 + 128)
                out_ref[:, at] = jnp.where(core == 0, ready[:half], ready[half:])
                send_ref[:, at] = jnp.where(core == 0, ready[half:], ready[:half])

    pl.when(step == 0)(functools.partial(work, 0, True, False))
    for parity in range(2):
        inner = (step > 0) & (step < pairs) & (lax.rem(step, 2) == parity)
        pl.when(inner)(functools.partial(work, parity, True, True))
    pl.when(step == pairs)(functools.partial(work, pairs % 2, False, True))


def attention(plan, segments, queries, mate_queries, w_uk, w_uv, mine, mate, state):
    half = queries.shape[0]
    rows = 2 * half
    heads = w_uk.shape[0]
    pairs = heads // 4
    last = pairs - 1
    diagonal = state is None
    blocks = 1 if diagonal else 2
    span = blocks * rows
    whole = lambda x: pl.BlockSpec(x.shape, lambda i, n: (0,) * x.ndim)
    pair = lambda i, n: n[0] * pairs + jnp.minimum(i, last)
    done = lambda i: jnp.maximum(i - 1, 0)
    query = pl.BlockSpec((half, 2 * (NOPE + ROPE)), lambda i, n: (0, pair(i, n)))
    part = pl.BlockSpec((2, rows, 128), lambda i, n: (done(i), 0, 0))
    coming = pl.BlockSpec((2, rows, 128), lambda i, n: (jnp.minimum(i, last), 0, 0))
    scratch = [
        pltpu.VMEM((2, 128), jnp.int32),
        pltpu.VMEM((span, LAT + ROPE), bf16),
        pltpu.VMEM((2, span, 128), bf16),
        pltpu.VMEM((2, rows, 256), bf16),
        *[pltpu.VMEM((2, span // 128, rows, 128), f32)] * 2,
        *[pltpu.VMEM((span, 256), bf16)] * 2,
        *[pltpu.VMEM((2, rows, 128), f32)] * 2,
    ]
    if diagonal:
        extra, more = [], []
        out_specs = [part] * 2
        out_shape = [jax.ShapeDtypeStruct((heads // 2, rows, 128), f32)] * 2
    else:
        extra, more = [part, coming], state
        scratch = [pltpu.VMEM((2, rows, 128), f32)] * 2 + scratch
        scratch += [pltpu.VMEM((2, rows, 128), f32)] * 2 + [pltpu.SMEM((2,), jnp.int32)]
        out_specs = [
            pl.BlockSpec((half, 2 * VDIM), lambda i, n: (0, n[0] * pairs + done(i))),
            pl.BlockSpec((half, 2 * VDIM), lambda i, n: (0, done(i))),
        ]
        out_shape = [
            jax.ShapeDtypeStruct((half, heads * VDIM), bf16),
            jax.ShapeDtypeStruct((half, heads * VDIM // 2), bf16),
        ]
    return pl.pallas_call(
        functools.partial(attention_kernel, diagonal, blocks, pairs),
        grid_spec=pltpu.PrefetchScalarGridSpec(
            num_scalar_prefetch=1,
            grid=(pairs + 1,),
            in_specs=[
                whole(segments),
                query,
                query,
                pl.BlockSpec((2, NOPE, LAT), lambda i, n: (pair(i, n), 0, 0)),
                pl.BlockSpec((2, LAT, VDIM), lambda i, n: (pair(i, n), 0, 0)),
                *[whole(x) for x in mine],
                *[whole(x) for x in mate],
                *extra,
            ],
            out_specs=out_specs,
            scratch_shapes=scratch,
        ),
        out_shape=out_shape,
        compiler_params=pltpu.CompilerParams(vmem_limit_bytes=60 << 20),
        cost_estimate=pl.CostEstimate(
            flops=16 << 30, bytes_accessed=16 << 20, transcendentals=rows * span * heads // 2
        ),
        name="diagonal_attention" if diagonal else "earlier_attention",
    )(plan, segments, queries, mate_queries, w_uk, w_uv, *mine, *mate, *more)


def swapped(x):
    size = lax.axis_size("ctx")
    return lax.ppermute(x, "ctx", [(i, i ^ 1) for i in range(size)])


def later(x, chips):
    size = lax.axis_size("ctx")
    return lax.ppermute(x, "ctx", [(i, i + 2 * chips) for i in range(size - 2 * chips)])


def around(x, by):
    size = lax.axis_size("head")
    return lax.ppermute(x, "head", [(i, (i + by) % size) for i in range(size)])


def everywhere(x):
    return [x, around(x, 1), around(x, -1), around(x, 2)]


def on_device(queries, latent, segments, w_uk, w_uv):
    half = queries.shape[0]
    rows = 2 * half
    owner = lax.axis_index("ctx")
    core = lax.rem(owner, 2)
    opening = (owner - core) * half
    plan = jnp.stack([core, lax.axis_index("head"), opening])
    segments = segments.reshape(-1, 128)

    mate_queries = swapped(queries)
    farther = later(latent, 2)
    mine = everywhere(latent)
    outgoing, mate_queries = lax.optimization_barrier((latent, mate_queries))
    nearer = later(outgoing, 1)
    mine, farther, nearer, mate_queries = lax.optimization_barrier(
        (mine, farther, nearer, mate_queries)
    )
    older = jnp.concatenate([farther, nearer])
    mate = [swapped(jnp.concatenate(mine))]
    older_mine = everywhere(older)
    state = attention(plan, segments, queries, mate_queries, w_uk, w_uv, mine, mate, None)
    older_mate = [swapped(older_mine[0])]
    state, arrived = lax.optimization_barrier((state, older_mine[1:]))
    older_mine = [older_mine[0], *arrived]
    older_mate += [swapped(x) for x in arrived]
    own, send = attention(
        plan, segments, queries, mate_queries, w_uk, w_uv, older_mine, older_mate, state
    )
    columns = send.shape[1]
    return lax.dynamic_update_slice(own, swapped(send), (0, (1 - core) * columns))


def solution(mesh):
    placed = (
        P(("dp", "ctx"), "head"),
        P(("dp", "ctx", "head"), None),
        P("dp"),
        P("head", None, None),
        P("head", None, None),
    )
    return jax.shard_map(
        on_device, mesh=mesh, in_specs=placed, out_specs=P(("dp", "ctx"), "head"), check_vma=False
    )
```

```python
import functools
import math

import jax
import jax.numpy as jnp
from jax import lax
from jax.experimental import pallas as pl
from jax.experimental.pallas import tpu as pltpu
from jax.sharding import PartitionSpec as P

NOPE = 128
ROPE = 64
LAT = 512
VDIM = 128
DOCS = 12
SCALE = math.log2(math.e) / math.sqrt(NOPE + ROPE)
FAR = -1e30
TILE = 256
WIDE = 512
NT = (((1,), (1,)), ((), ()))
f32, bf16 = jnp.float32, jnp.bfloat16


def attention_kernel(diagonal, blocks, pairs, *refs):
    plan_ref, segment_ref, own_q, mate_q, uk_ref, uv_ref = refs[:6]
    mine = refs[6:10]
    if diagonal:
        piece = mine[0].shape[0]
        mate = [refs[10].at[k * piece : (k + 1) * piece] for k in range(4)]
        refs = refs[11:]
    else:
        mate, refs = refs[10:14], refs[14:]
    if diagonal:
        out_mean, out_weight = refs[:2]
        refs = refs[2:]
    else:
        in_mean, in_weight, out_ref, send_ref = refs[:4]
        weight_refs, refs = refs[4:6], refs[6:]
        sum_ref, total_ref, bound_ref = refs[10:]
    edges_ref, lat_ref, tail_ref, qcat_ref = refs[:4]
    score_refs, value_refs, top_refs = refs[4:6], refs[6:8], refs[8:10]
    step = pl.program_id(0)
    half = own_q.shape[0]
    rows = 2 * half
    past = 2 * rows
    base = past if diagonal else 0
    core, column = plan_ref[0], plan_ref[1]

    @pl.when(step == 0)
    def _():
        piece = mine[0].shape[0] // blocks
        for kind, group in ((core, mine), (1 - core, mate)):
            for ring, ref in zip((0, 3, 1, 2), group):
                slot = lax.rem(column + ring, 4)
                for block in range(blocks):
                    first = pl.multiple_of(block * rows + kind * half + slot * piece, 16)
                    lat_ref[pl.ds(first, piece), :] = ref[block * piece : (block + 1) * piece]
        segment = segment_ref[...]
        below = [jnp.sum(jnp.where(segment < doc, 1.0, 0.0)) for doc in range(1, DOCS)]
        below = [0.0, *below, float(segment.size)]
        label = lax.broadcasted_iota(jnp.int32, (1, 128), 1) & 63
        lows = highs = jnp.full((1, 128), below[DOCS], f32)
        for doc in range(DOCS):
            lows = jnp.where(label == doc, below[doc], lows)
            highs = jnp.where(label == doc, below[doc + 1], highs)
        opening = (plan_ref[2] - past).astype(f32)
        lows, highs = lows - opening, highs - opening
        edges_ref[:1] = lows.astype(jnp.int32)
        edges_ref[1:] = highs.astype(jnp.int32)
        keys = lat_ref.shape[0]
        rope = lat_ref[:, LAT:].astype(f32) * SCALE
        at = lax.broadcasted_iota(jnp.int32, (keys, ROPE), 0) + base
        inside = (at >= edges_ref[:1, :ROPE]) & (at < edges_ref[1:, :ROPE])
        far = jnp.where(inside, 0.0, FAR).astype(f32)
        tail_ref[0] = jnp.concatenate([rope, far], axis=1).astype(bf16)
        tail_ref[1] = jnp.concatenate([far, rope], axis=1).astype(bf16)
        if not diagonal:
            begin = jnp.max(jnp.where(lows <= past, lows, -1e9)).astype(jnp.int32)
            finish = jnp.min(jnp.where(highs > past, highs, 1e9)).astype(jnp.int32)
            bound_ref[0] = lax.div(past - begin + TILE - 1, TILE)
            bound_ref[1] = finish - past

    def scores(head, first, size, keys, low, high):
        joined = jnp.concatenate(
            [keys[:, head * 128 : head * 128 + 128], tail_ref[head, pl.ds(first, size), :]], axis=1
        )
        return lax.dot_general(qcat_ref[head, low:high], joined, NT, preferred_element_type=f32)

    def keep(now, head, first, low, high, score, fresh):
        parts = [score[:, k : k + 128] for k in range(0, score.shape[1], 128)]
        best = parts[0]
        for part in parts[1:]:
            best = jnp.maximum(best, part)
        if not fresh:
            best = jnp.maximum(top_refs[now][head, low:high], best)
        top_refs[now][head, low:high] = best
        for k, part in enumerate(parts):
            score_refs[now][head, first // 128 + k, low:high] = part

    def project(now, first, size, wide_uk, wide_uv):
        piece = lat_ref[pl.ds(first, size), :LAT]
        keys = lax.dot_general(piece, wide_uk, NT, preferred_element_type=f32)
        values = jnp.dot(piece, wide_uv, preferred_element_type=f32)
        value_refs[now][pl.ds(first, size), :] = values.astype(bf16)
        return (keys * SCALE).astype(bf16)

    def weigh(before, head, first, size, low, high):
        top = top_refs[before][head, low:high]
        weights = [
            jnp.exp2(score_refs[before][head, first // 128 + k, low:high] - top)
            for k in range(size // 128)
        ]
        values = value_refs[before][pl.ds(first, size), head * 128 : head * 128 + 128]
        both = jnp.dot(
            jnp.concatenate([x.astype(bf16) for x in weights], axis=1),
            jnp.concatenate([values, jnp.ones((size, 128), bf16)], axis=1),
            preferred_element_type=f32,
        )
        return both[:, :128], both[:, 128:]

    def work(now, projecting, weighing):
        before = 1 - now
        if projecting:
            lane = lax.broadcasted_iota(jnp.int32, (rows, 128), 1)
            small = lane < 64
            at = lax.broadcasted_iota(jnp.int32, (rows, 128), 0) + past
            inside = (at >= edges_ref[:1]) & (at < edges_ref[1:])
            doc = jnp.where(inside, 1.0, 0.0).astype(bf16)
            own, other = own_q[...], mate_q[...]
            lead = core == 0
            whole = jnp.concatenate(
                [jnp.where(lead, own, other), jnp.where(lead, other, own)], axis=0
            )
            left, mid, right = whole[:, :128], whole[:, 128:256], whole[:, 256:]
            qcat_ref[0] = jnp.concatenate([left, jnp.where(small, mid, doc)], axis=1)
            qcat_ref[1] = jnp.concatenate(
                [jnp.where(small, right, mid), jnp.where(small, doc, right)], axis=1
            )
            wide_uk = jnp.concatenate([uk_ref[0], uk_ref[1, 64:], uk_ref[1, :64]], axis=0)
            wide_uv = jnp.concatenate([uv_ref[0], uv_ref[1]], axis=1)
        if diagonal:
            for low in range(0, rows, TILE):
                for head in range(2 if weighing else 0):
                        high = low + TILE
                        sums, total = weigh(before, head, 0, high, low, high)
                        out_mean[head, low:high] = sums * (1.0 / total)
                        out_weight[head, low:high] = top_refs[before][head, low:high] + jnp.log2(total)
            if projecting:
                keys = project(now, 0, rows, wide_uk, wide_uv)
            for low in range(0, rows, TILE):
                for head in range(2 if projecting else 0):
                        score = scores(head, low, TILE, keys[low : low + TILE], low, rows)
                        row = lax.broadcasted_iota(jnp.int32, (TILE, TILE), 0)
                        col = lax.broadcasted_iota(jnp.int32, (TILE, TILE), 1)
                        edge = jnp.where(col <= row, score[:TILE], FAR)
                        if low + TILE < rows:
                            edge = jnp.concatenate([edge, score[TILE:]], axis=0)
                        keep(now, head, low, low, rows, edge, low == 0)
        else:
            for head in range(2):
                if projecting:
                    top_refs[now][head] = in_weight[head]
                    weight_refs[now][head] = in_weight[head]
                if weighing:
                    scale = jnp.exp2(weight_refs[before][head] - top_refs[before][head])
                    sum_ref[head] = in_mean[head] * scale
                    total_ref[head] = scale

            def earlier(high):
                def tile(first, size):
                    for head in range(2 if weighing else 0):
                        sums, total = weigh(before, head, first, size, 0, high)
                        sum_ref[head, :high] = sum_ref[head, :high] + sums
                        total_ref[head, :high] = total_ref[head, :high] + total
                    if projecting:
                        keys = project(now, first, size, wide_uk, wide_uv)
                    for head in range(2 if projecting else 0):
                        score = scores(head, first, size, keys, 0, high)
                        keep(now, head, first, 0, high, score, False)

                def wide(turn, carry):
                    tile(pl.multiple_of(past - (turn + 1) * WIDE, WIDE), WIDE)
                    return carry

                def rest(turn, carry):
                    tile(pl.multiple_of(past - bound_ref[0] * TILE, TILE), TILE)
                    return carry

                lax.fori_loop(0, lax.div(bound_ref[0], WIDE // TILE), wide, 0)
                lax.fori_loop(0, lax.rem(bound_ref[0], WIDE // TILE), rest, 0)

            reach = bound_ref[1]
            for high in range(TILE, rows + 1, TILE):
                fits = reach > high - TILE
                if high < rows:
                    fits = fits & (reach <= high)
                pl.when(fits)(functools.partial(earlier, high))

        if projecting:
            for head in range(2):
                best = jnp.max(top_refs[now][head], axis=1, keepdims=True)
                top_refs[now][head] = jnp.broadcast_to(best, (rows, 128))
        if weighing and not diagonal:
            for head in range(2):
                ready = (sum_ref[head] * (1.0 / total_ref[head])).astype(bf16)
                at = slice(head * 128, head * 128 + 128)
                out_ref[:, at] = jnp.where(core == 0, ready[:half], ready[half:])
                send_ref[:, at] = jnp.where(core == 0, ready[half:], ready[:half])

    pl.when(step == 0)(functools.partial(work, 0, True, False))
    for parity in range(2):
        inner = (step > 0) & (step < pairs) & (lax.rem(step, 2) == parity)
        pl.when(inner)(functools.partial(work, parity, True, True))
    pl.when(step == pairs)(functools.partial(work, pairs % 2, False, True))


def attention(plan, segments, queries, mate_queries, w_uk, w_uv, mine, mate, state):
    half = queries.shape[0]
    rows = 2 * half
    heads = w_uk.shape[0]
    pairs = heads // 4
    last = pairs - 1
    diagonal = state is None
    blocks = 1 if diagonal else 2
    span = blocks * rows
    whole = lambda x: pl.BlockSpec(x.shape, lambda i, n: (0,) * x.ndim)
    pair = lambda i, n: n[0] * pairs + jnp.minimum(i, last)
    done = lambda i: jnp.maximum(i - 1, 0)
    query = pl.BlockSpec((half, 2 * (NOPE + ROPE)), lambda i, n: (0, pair(i, n)))
    part = pl.BlockSpec((2, rows, 128), lambda i, n: (done(i), 0, 0))
    coming = pl.BlockSpec((2, rows, 128), lambda i, n: (jnp.minimum(i, last), 0, 0))
    scratch = [
        pltpu.VMEM((2, 128), jnp.int32),
        pltpu.VMEM((span, LAT + ROPE), bf16),
        pltpu.VMEM((2, span, 128), bf16),
        pltpu.VMEM((2, rows, 256), bf16),
        *[pltpu.VMEM((2, span // 128, rows, 128), f32)] * 2,
        *[pltpu.VMEM((span, 256), bf16)] * 2,
        *[pltpu.VMEM((2, rows, 128), f32)] * 2,
    ]
    if diagonal:
        extra, more = [], []
        out_specs = [part] * 2
        out_shape = [jax.ShapeDtypeStruct((heads // 2, rows, 128), f32)] * 2
    else:
        extra, more = [part, coming], state
        scratch = [pltpu.VMEM((2, rows, 128), f32)] * 2 + scratch
        scratch += [pltpu.VMEM((2, rows, 128), f32)] * 2 + [pltpu.SMEM((2,), jnp.int32)]
        out_specs = [
            pl.BlockSpec((half, 2 * VDIM), lambda i, n: (0, n[0] * pairs + done(i))),
            pl.BlockSpec((half, 2 * VDIM), lambda i, n: (0, done(i))),
        ]
        out_shape = [
            jax.ShapeDtypeStruct((half, heads * VDIM), bf16),
            jax.ShapeDtypeStruct((half, heads * VDIM // 2), bf16),
        ]
    return pl.pallas_call(
        functools.partial(attention_kernel, diagonal, blocks, pairs),
        grid_spec=pltpu.PrefetchScalarGridSpec(
            num_scalar_prefetch=1,
            grid=(pairs + 1,),
            in_specs=[
                whole(segments),
                query,
                query,
                pl.BlockSpec((2, NOPE, LAT), lambda i, n: (pair(i, n), 0, 0)),
                pl.BlockSpec((2, LAT, VDIM), lambda i, n: (pair(i, n), 0, 0)),
                *[whole(x) for x in mine],
                *[whole(x) for x in mate],
                *extra,
            ],
            out_specs=out_specs,
            scratch_shapes=scratch,
        ),
        out_shape=out_shape,
        compiler_params=pltpu.CompilerParams(vmem_limit_bytes=(60 if diagonal else 48) << 20),
        cost_estimate=pl.CostEstimate(
            flops=16 << 30, bytes_accessed=16 << 20, transcendentals=rows * span * heads // 2
        ),
        name="diagonal_attention" if diagonal else "earlier_attention",
    )(plan, segments, queries, mate_queries, w_uk, w_uv, *mine, *mate, *more)


def swapped(x):
    size = lax.axis_size("ctx")
    return lax.ppermute(x, "ctx", [(i, i ^ 1) for i in range(size)])


def later(x, chips):
    size = lax.axis_size("ctx")
    return lax.ppermute(x, "ctx", [(i, i + 2 * chips) for i in range(size - 2 * chips)])


def around(x, by):
    size = lax.axis_size("head")
    return lax.ppermute(x, "head", [(i, (i + by) % size) for i in range(size)])


def everywhere(x):
    return [x, around(x, 1), around(x, -1), around(x, 2)]


def on_device(queries, latent, segments, w_uk, w_uv):
    half = queries.shape[0]
    rows = 2 * half
    owner = lax.axis_index("ctx")
    core = lax.rem(owner, 2)
    opening = (owner - core) * half
    plan = jnp.stack([core, lax.axis_index("head"), opening])
    segments = segments.reshape(-1, 128)

    mate_queries = swapped(queries)
    farther = later(latent, 2)
    mine = everywhere(latent)
    outgoing, mate_queries = lax.optimization_barrier((latent, mate_queries))
    nearer = later(outgoing, 1)
    mine, farther, nearer, mate_queries = lax.optimization_barrier(
        (mine, farther, nearer, mate_queries)
    )
    older = jnp.concatenate([farther, nearer])
    mate = [swapped(jnp.concatenate(mine))]
    older_mine = everywhere(older)
    state = attention(plan, segments, queries, mate_queries, w_uk, w_uv, mine, mate, None)
    older_mate = [swapped(older_mine[0])]
    state, arrived = lax.optimization_barrier((state, older_mine[1:]))
    older_mine = [older_mine[0], *arrived]
    older_mate += [swapped(x) for x in arrived]
    own, send = attention(
        plan, segments, queries, mate_queries, w_uk, w_uv, older_mine, older_mate, state
    )
    columns = send.shape[1]
    return lax.dynamic_update_slice(own, swapped(send), (0, (1 - core) * columns))


def solution(mesh):
    placed = (
        P(("dp", "ctx"), "head"),
        P(("dp", "ctx", "head"), None),
        P("dp"),
        P("head", None, None),
        P("head", None, None),
    )
    return jax.shard_map(
        on_device, mesh=mesh, in_specs=placed, out_specs=P(("dp", "ctx"), "head"), check_vma=False
    )
```
